512 devices in a mesh: seq: 32 (over x, z_lo), fsdp: 16 (over y, z_hi, core).
Axes of the slice: x: 4, y: 4, z: 16 (z_hi: 2, z_lo: 8; z = z_hi * 8 + z_lo), core: 2. Of those that a mesh axis runs over, the one named last changes fastest.
Arguments:
- qkv: bfloat16 [16, 8192, 6144], P('fsdp', 'seq'), may hold values from -6 to 6
- resid: bfloat16 [16, 8192, 2048], P('fsdp', 'seq'), may hold values from -40 to 40
- targets: int32 [16, 8192], P('fsdp', 'seq'), may hold values from 0 to 511
- short_filter: float32 [7, 6144], replicated, may hold values from -2 to 2
- long_filter: bfloat16 [128, 128], replicated, may hold values from -0.5 to 0.5
- skip: float32 [2048], replicated, may hold values from -3 to 3
- out_weight: bfloat16 [2048, 2048], P('fsdp'), may hold values from -0.125 to 0.125
- gain: float32 [2048], replicated, may hold values from 0.1 to 1.9
- vocab_weight: bfloat16 [512, 2048], P('fsdp'), may hold values from -64 to 64
Outputs:
- logprob: float32 [16, 8192], P('fsdp', 'seq')
The draws below stay inside these ranges and needn't reach their ends.
All inputs are finite; a program needn't handle non-finite values.
Results may differ from the reference program's by a relative error of at most 0.0022.
Values may be sent and summed in bfloat16 or wider, within the bound.
A program may use at most 128 MiB of HBM per device.

```python
import math
import jax
import jax.numpy as jnp
import numpy as np
from jax import lax

H = 2048
DOUT = 2048
VOCAB = 512
G = 128
WINDOWS = 16
LENGTH = 8192


def draw_resid(key, part):
    key = jax.random.fold_in(key, 11)
    key_base, key_rows, key_cols = jax.random.split(key, 3)
    shape = (WINDOWS, LENGTH, DOUT)
    base = jax.random.normal(key_base, shape, jnp.float32)
    rows = jnp.exp(jax.random.uniform(key_rows, (WINDOWS, LENGTH, 1), jnp.float32, jnp.log(0.3), jnp.log(3.0)))
    cols = jnp.exp(jax.random.uniform(key_cols, (1, 1, DOUT), jnp.float32, jnp.log(0.3), jnp.log(3.0)))
    return jnp.clip(base * rows * cols, -40.0, 40.0).astype(jnp.bfloat16)


def draw_vocab_weight(key, part):
    key = jax.random.fold_in(key, 23)
    key_base = jax.random.fold_in(key, 0)
    spread = 3.0 / DOUT ** 0.5
    base = jax.random.normal(key_base, (VOCAB, DOUT), jnp.float32) * spread
    return jnp.clip(base, -64.0, 64.0).astype(jnp.bfloat16)


def place_ends(drawn, rng, smallest, high):
    index_at = [jax.random.randint(jax.random.fold_in(rng, axis), (), 0, length) for axis, length in enumerate(drawn.shape)]
    main_axis = drawn.shape.index(max(drawn.shape))
    next_to = index_at[:main_axis] + [(index_at[main_axis] + 1) % drawn.shape[main_axis]] + index_at[main_axis + 1:]
    return drawn.at[tuple(index_at)].set(smallest).at[tuple(next_to)].set(high)


def block_scale(key, shape, cuts, low, largest):
    level = 1.0
    for dim, parts in cuts:
        heights = jax.random.uniform(jax.random.fold_in(jax.random.fold_in(key, 6), dim), (parts,), jnp.float32, low / len(cuts), largest / len(cuts))
        level = level * jnp.repeat(jnp.exp(heights), shape[dim] // parts).reshape((-1,) + (1,) * (len(shape) - 1 - dim))
    return level


def rank_table(count, slope):
    loads = [(1 << 20) // math.isqrt(grade ** slope) + 1 for grade in range(1, count + 1)]
    deviation = 1 + sum(loads) // (1 << 30)
    return np.cumsum(np.array([max(1, weight // deviation) for weight in loads]))


def ranked(rng, extent, amount, skew):
    listing = rank_table(amount, skew)
    pick = jax.random.randint(jax.random.fold_in(rng, 1), extent, 0, int(listing[amount - 1]))
    grade = jnp.searchsorted(jnp.asarray(listing, jnp.int32), pick, side="right")
    return jax.random.permutation(jax.random.fold_in(rng, 2), amount)[grade].astype(jnp.int32)


def gaussian(own_key, extent, scale, most, cuts=(), held_as=jnp.bfloat16):
    entries = jax.random.normal(own_key, extent, jnp.float32) * scale
    if len(cuts) > 0:
        entries = block_scale(own_key, extent, cuts, -0.22, 0.18) * entries
    return jnp.clip(entries, min=-most, max=most).astype(held_as)


def setup_inputs(seed: int = 0) -> dict:
    streams_of = jax.random.split(jax.random.key(seed), 10)
    qkv = gaussian(streams_of[0], (WINDOWS, LENGTH, 3 * H), 1.0, 6.0, ((0, 16), (1, 32)))
    resid = draw_resid(jax.random.fold_in(streams_of[9], 71), 0)
    targets = place_ends(ranked(streams_of[2], (WINDOWS, LENGTH), VOCAB, 2), jax.random.fold_in(streams_of[2], 3), 0, VOCAB - 1).astype(jnp.int32)
    short_filter = gaussian(streams_of[3], (7, 3 * H), 7 ** -0.5, 2.0, (), jnp.float32)
    long_filter = gaussian(streams_of[4], (G, 128), 128 ** -0.5, 0.5)
    skip = gaussian(streams_of[5], (H,), 0.5, 3.0, (), jnp.float32)
    out_weight = gaussian(streams_of[6], (H, DOUT), H ** -0.5, 0.125, ((0, 16),))
    gain = jnp.clip(1.0 + 0.18 * jax.random.normal(streams_of[7], (DOUT,), jnp.float32), 0.1, 1.9)
    vocab_weight = draw_vocab_weight(jax.random.fold_in(streams_of[9], 71), 0)
    return {"qkv": qkv, "resid": resid, "targets": targets, "short_filter": short_filter, "long_filter": long_filter, "skip": skip, "out_weight": out_weight, "gain": gain, "vocab_weight": vocab_weight}


def short_conv(extended, taps):
    count = extended.shape[0] - 6
    total = jnp.zeros((count, extended.shape[1]), jnp.float32)
    for lag in range(7):
        total = total + taps[lag] * extended[6 - lag:6 - lag + count].astype(jnp.float32)
    return total

def toeplitz(taps):
    groups = taps.shape[0]
    flipped = taps[:, ::-1]
    padded = jnp.concatenate([jnp.zeros((groups, 1), taps.dtype), flipped, jnp.zeros((groups, 128), taps.dtype)], axis=1)
    tiled = jnp.tile(padded, (1, 128))[:, :128 * 256]
    return tiled.reshape(groups, 128, 256)

def long_conv(extended, matrix):
    blocks = extended.shape[0] // 128 - 1
    channels = extended.shape[1]
    groups = matrix.shape[0]
    pieces = extended.reshape(blocks + 1, 128, groups, channels // groups)
    pairs = jnp.concatenate([pieces[:-1], pieces[1:]], axis=1)
    result = jnp.einsum('gij,bjgc->bigc', matrix.astype(jnp.float32), pairs.astype(jnp.float32))
    return result.reshape(blocks * 128, channels)

def one_window(rows, stream_in, wanted, short_filter, matrix, skip, out_weight, gain, vocab_weight):
    hidden = skip.shape[0]
    extended = jnp.concatenate([jnp.zeros((6, rows.shape[1]), rows.dtype), rows], axis=0)
    feat = short_conv(extended, short_filter)
    query = feat[:, :hidden]
    product = (feat[:, hidden:2 * hidden] * feat[:, 2 * hidden:]).astype(jnp.bfloat16)
    longer = jnp.concatenate([jnp.zeros((128, hidden), jnp.bfloat16), product], axis=0)
    wave = long_conv(longer, matrix) + skip * product.astype(jnp.float32)
    gated = (query * wave).astype(jnp.bfloat16)
    stream = stream_in.astype(jnp.float32) + jnp.dot(gated, out_weight, preferred_element_type=jnp.float32)
    scale = lax.rsqrt(lax.optimization_barrier(jnp.mean(stream * stream, axis=-1, keepdims=True)) + 1e-05)
    normed = (stream * scale * gain).astype(jnp.bfloat16)
    logits = jnp.dot(normed, vocab_weight.T, preferred_element_type=jnp.float32)
    top = lax.optimization_barrier(jnp.max(logits, axis=-1, keepdims=True))
    total = top[:, 0] + jnp.log(lax.optimization_barrier(jnp.sum(jnp.exp(logits - top), axis=-1)))
    column = lax.broadcasted_iota(jnp.int32, logits.shape, 1)
    picked = lax.optimization_barrier(jnp.sum(jnp.where(column == wanted[:, None].astype(jnp.int32), logits, 0.0), axis=-1))
    return picked - total

def reference(qkv, resid, targets, short_filter, long_filter, skip, out_weight, gain, vocab_weight):
    matrix = toeplitz(long_filter)

    def window(items):
        return one_window(items[0], items[1], items[2], short_filter, matrix, skip, out_weight, gain, vocab_weight)
    return lax.map(window, (qkv, resid, targets))
```

```python
import jax
import jax.numpy as jnp
from jax import lax
from jax.experimental import pallas as pl
from jax.experimental.pallas import tpu as pltpu
from jax.sharding import PartitionSpec as P

MESH = pl.DeviceIdType.MESH
BF = jnp.bfloat16
F32 = jnp.float32


def place(x, y, z, c):
    x, y, z = lax.rem(x + 4, 4), lax.rem(y + 4, 4), lax.rem(z + 16, 16)
    return (x * 8 + lax.rem(z, 8), (y * 2 + z // 8) * 2 + c)


def cols(start, size):
    return pl.ds(pl.multiple_of(start, 128), size)


def kernel(
    qkv, resid, targets, taps, longs, skip, ow, gain, vw, out,
    raw, ext, prod, query, flips, mats, gated, wbuf, vbuf, stream, base, local_sem, send_sem, recv_sem,
):
    s, f = lax.axis_index("seq"), lax.axis_index("fsdp")
    x, zl = s // 8, lax.rem(s, 8)
    y, h, c = f // 4, lax.rem(f // 2, 2), lax.rem(f, 2)
    o = 1 - h
    z = h * 8 + zl
    lo, hi = zl == 0, zl == 7
    xl, xs, yl, ys = 1 - c, c, c, 1 - c

    def longer(d):
        return place(x + d * xl, y + d * yl, z, c)

    def shorter(d):
        return place(x + d * xs, y + d * ys, z, c)

    sibling = (s, f + 1 - 2 * c)
    after, before = (lax.rem(s + 1, 32), f), (lax.rem(s + 31, 32), f)
    source = place(x, y, jnp.where(zl < 4, h * 8 - 1, h * 8 + 8), c)

    def across(d):
        return place(x, y, jnp.where(lo, z - d, z + d), c)

    edge = jnp.logical_or(lo, hi)

    barrier = pltpu.get_barrier_semaphore()

    def greet(device):
        pl.semaphore_signal(barrier, inc=1, device_id=device, device_id_type=MESH)

    for d in (1, 2, 3):
        greet(longer(d))
        greet(shorter(d))
    for device in (sibling, after, before, source):
        greet(device)

    @pl.when(edge)
    def _():
        for d in (1, 2, 3, 4):
            greet(across(d))

    def load(src, dst, k):
        copy = pltpu.make_async_copy(src, dst, local_sem.at[k])
        copy.start()
        return copy

    H = 2048
    load_k = load(qkv.at[0, :, H : 2 * H], raw.at[16:272, H : 2 * H], 0)
    load_v = load(qkv.at[0, :, 2 * H :], raw.at[16:272, 2 * H :], 1)
    load_q = load(qkv.at[0, :, :H], raw.at[16:272, :H], 2)
    load_w = load(ow, wbuf.at[y, h, c], 3)
    load_u = load(vw, vbuf.at[y, h, c], 4)
    load_r = load(resid.at[0], base, 5)

    count = [0]
    sent = []

    def send(pairs, device, slot=None):
        copies = []
        for k, (src, dst) in enumerate(pairs):
            n = count[0]
            count[0] += 1
            copies.append(
                pltpu.make_async_remote_copy(
                    src_ref=src, dst_ref=dst, send_sem=send_sem.at[n],
                    recv_sem=recv_sem.at[n if slot is None else slot + k],
                    device_id=device, device_id_type=MESH,
                )
            )
        return copies

    def start(copies):
        for copy in copies:
            copy.start()

    def arrive(copies):
        for copy in copies:
            copy.wait_recv()

    def leave(copies):
        for copy in copies:
            copy.wait_send()

    quarter = cols(x * 512, 512)
    mine = [(ow, wbuf.at[y, h, c]), (vw, vbuf.at[y, h, c])]

    def block(yy, hh):
        return [(b.at[yy, hh, c], b.at[yy, hh, c]) for b in (wbuf, vbuf)]

    def part(yy, hh, xx):
        k = cols(xx * 512, 512)
        return [(b.at[yy, hh, c, :, k], b.at[yy, hh, c, :, k]) for b in (wbuf, vbuf)]

    def column(hh, xx):
        k = cols(xx * 512, 512)
        return [(b.at[:, hh, c, :, k], b.at[:, hh, c, :, k]) for b in (wbuf, vbuf)]

    def back(a, d):
        return lax.rem(a + 4 - d, 4)

    quarter_mine = [(ow.at[:, quarter], wbuf.at[y, h, c, :, quarter]), (vw.at[:, quarter], vbuf.at[y, h, c, :, quarter])]

    edge_slot = count[0]
    cross = [send(quarter_mine, across(d), edge_slot) for d in (4, 3, 2, 1)]
    cross_in = send(part(y, o, x), source, edge_slot)
    heads = send([(qkv.at[0, 240:256], raw.at[0:16])], after)
    full = {d: send(mine, longer(d)) for d in (1, 3, 2)}
    first = {d: send(quarter_mine, shorter(d)) for d in (1, 3, 2)}
    second = {(k, d): send(part(back(y, k), h, x), longer(d)) for k in (1, 3, 2) for d in (1, 3, 2)}
    tails = send([(prod.at[256:384], prod.at[0:128])], after)
    spread = {d: send(part(y, o, x), shorter(d)) for d in (1, 3, 2)}
    wide0 = {d: send(column(o, x), longer(d)) for d in (1, 3, 2)}
    wide1 = {d: send(block(y, o), longer(d)) for d in (1, 3, 2)}
    mate = send(mine, sibling)
    mate_own = {d: send(block(back(y, d), h), sibling) for d in (1, 3, 2)}
    mate_cross0 = {d: send(column(o, back(x, d)), sibling) for d in (0, 1, 3, 2)}
    slots = count[0]
    mate_cross1 = {}
    for d in (0, 1, 3, 2):
        n = count[0]
        mate_cross1[d] = send(block(back(y, d), o), sibling)

    pl.semaphore_wait(barrier, 10 + jnp.where(edge, 4, 0))

    @pl.when(edge)
    def _():
        for copies in cross:
            start(copies)

    start(heads)

    @pl.when(c == 0)
    def _():
        for d in (1, 3, 2):
            start(first[d])

    @pl.when(c == 1)
    def _():
        for d in (1, 3, 2):
            start(full[d])

    start(mate)

    def conv(col, lane, top, spot):
        ext[spot] = raw[top : top + 144, cols(col, 128)].astype(F32)
        total = jnp.zeros((128, 128), F32)
        for lag in range(7):
            total = total + taps[lag : lag + 1, cols(col, 128)] * ext[spot, 16 - lag : 144 - lag]
        return total

    def product(j, top):
        lane = j * 128
        k = conv(H + lane, lane, top, 0)
        v = conv(2 * H + lane, lane, top, 1)
        prod[128 + top : 256 + top, cols(lane, 128)] = (k * v).astype(BF)

    load_k.wait()
    load_v.wait()

    @pl.loop(0, 16)
    def _(j):
        product(j, 128)

    start(tails)
    load_q.wait()
    arrive(heads)

    @pl.when(s == 0)
    def _():
        raw[0:16] = jnp.zeros((16, 3 * H), BF)

    @pl.when(c == 0)
    def _():
        for d in (1, 3, 2):
            arrive(first[d])
            for e in (1, 3, 2):
                start(second[d, e])

    @pl.loop(0, 16)
    def _(j):
        product(j, 0)
        lane = j * 128
        query[0:128, cols(lane, 128)] = conv(lane, lane, 0, 2)
        query[128:256, cols(lane, 128)] = conv(lane, lane, 128, 3)

    rows = lax.broadcasted_iota(jnp.int32, (128, 128), 0)
    lanes = lax.broadcasted_iota(jnp.int32, (128, 128), 1)
    turn = jnp.where(lax.rem(rows + lanes, 128) == 0, 1.0, 0.0).astype(BF)
    flips[...] = jnp.dot(longs[...], turn, preferred_element_type=F32)

    @pl.loop(0, 128)
    def _(g):
        spin = pltpu.roll(jnp.broadcast_to(flips[pl.ds(g, 1), :], (128, 128)), 0, 1, stride=1, stride_axis=0)
        at = pl.ds(pl.multiple_of(g * 128, 128), 128)
        mats[at, 0:128] = jnp.where(lanes > rows, spin, 0.0).astype(BF)
        mats[at, 128:256] = jnp.where(lanes > rows, 0.0, spin).astype(BF)

    arrive(cross_in)
    for d in (1, 3, 2):
        start(spread[d])

    @pl.when(c == 0)
    def _():
        for d in (1, 3, 2):
            for k in (1, 3, 2):
                arrive(second[k, d])
        for d in (1, 3, 2):
            start(mate_own[d])
        for d in (1, 3, 2):
            arrive(spread[d])
        for d in (1, 3, 2):
            start(wide0[d])
        start(mate_cross0[0])

    @pl.when(c == 1)
    def _():
        for d in (1, 3, 2):
            arrive(full[d])
            start(mate_own[d])
        for d in (1, 3, 2):
            arrive(spread[d])
        for d in (1, 3, 2):
            start(wide1[d])
        start(mate_cross1[0])

    arrive(tails)

    @pl.when(s == 0)
    def _():
        prod[0:128] = jnp.zeros((128, H), BF)

    group = lax.broadcasted_iota(jnp.int32, (128, 128), 1) // 16

    @pl.loop(0, 16)
    def _(j):
        lane = cols(j * 128, 128)
        pair = jnp.concatenate([prod[0:256, lane], prod[128:384, lane]], axis=1)
        spans = jnp.dot(mats[pl.ds(pl.multiple_of(j * 1024, 1024), 1024), :], pair, preferred_element_type=F32)
        for b in (0, 1):
            wave = spans[0:128, b * 128 : b * 128 + 128]
            for g in range(1, 8):
                wave = jnp.where(group == g, spans[g * 128 : g * 128 + 128, b * 128 : b * 128 + 128], wave)
            at = slice(b * 128, b * 128 + 128)
            wave = wave + skip[:, lane] * prod[b * 128 + 128 : b * 128 + 256, lane].astype(F32)
            gated[at, lane] = (query[at, lane] * wave).astype(BF)

    load_w.wait()
    load_u.wait()
    load_r.wait()

    def project(hh, n):
        total = None
        for yy in range(4):
            left = gated[:, cols((yy * 2 + hh) * 256, 256)]
            right = wbuf[yy, hh, :, :, cols(n * 256, 256)].reshape(256, 256)
            term = jnp.dot(left, right, preferred_element_type=F32)
            total = term if total is None else total + term
        return total

    arrive(mate)
    for d in (1, 3, 2):
        arrive(mate_own[d])

    @pl.loop(0, 8)
    def _(n):
        at = cols(n * 256, 256)
        stream[:, at] = base[:, at].astype(F32) + project(h, n)

    @pl.when(c == 0)
    def _():
        for d in (1, 3, 2):
            arrive(wide0[d])
            start(mate_cross0[d])
        for d in (0, 1, 3, 2):
            arrive(mate_cross1[d])

    @pl.when(c == 1)
    def _():
        for d in (1, 3, 2):
            arrive(wide1[d])
            start(mate_cross1[d])
        for d in (0, 1, 3, 2):
            arrive(mate_cross0[d])

    def close(n, squares):
        at = cols(n * 256, 256)
        total = stream[:, at] + project(o, n)
        stream[:, at] = total
        return squares + total[:, :128] * total[:, :128] + total[:, 128:] * total[:, 128:]

    squares = lax.fori_loop(0, 8, close, jnp.zeros((256, 128), F32))
    scale = lax.rsqrt(jnp.sum(squares, axis=1, keepdims=True) / 2048.0 + 1e-05)

    @pl.loop(0, 8)
    def _(n):
        at = cols(n * 256, 256)
        gated[:, at] = (stream[:, at] * scale * gain[:, at]).astype(BF)

    logits = lax.dot_general(
        vbuf[...].reshape(512, H), gated[...], (((1,), (1,)), ((), ())), preferred_element_type=F32
    )
    top = jnp.max(logits, axis=0, keepdims=True)
    total = top + jnp.log(jnp.sum(jnp.exp(logits - top), axis=0, keepdims=True))
    entry = lax.broadcasted_iota(jnp.int32, (512, 256), 0)
    out[...] = jnp.sum(jnp.where(entry == targets[...], logits, 0.0), axis=0, keepdims=True) - total

    @pl.when(edge)
    def _():
        for copies in cross:
            leave(copies)

    leave(heads)
    leave(tails)
    leave(mate)
    for d in (1, 2, 3):
        leave(spread[d])
        leave(mate_own[d])

    @pl.when(c == 0)
    def _():
        for d in (1, 3, 2):
            leave(first[d])
            for e in (1, 3, 2):
                leave(second[d, e])
            leave(wide0[d])
        for d in (0, 1, 2, 3):
            leave(mate_cross0[d])

    @pl.when(c == 1)
    def _():
        for d in (1, 3, 2):
            leave(full[d])
            leave(wide1[d])
        for d in (0, 1, 2, 3):
            leave(mate_cross1[d])


def body(qkv, resid, targets, short_filter, long_filter, skip, out_weight, gain, vocab_weight):
    vmem = pl.BlockSpec(memory_space=pltpu.VMEM)
    hbm = pl.BlockSpec(memory_space=pl.ANY)
    return pl.pallas_call(
        kernel,
        name="hyena_block",
        out_shape=jax.ShapeDtypeStruct((1, 256), F32),
        in_specs=[hbm, hbm, vmem, vmem, vmem, vmem, hbm, vmem, hbm],
        out_specs=vmem,
        scratch_shapes=[
            pltpu.VMEM((272, 6144), BF),
            pltpu.VMEM((4, 144, 128), F32),
            pltpu.VMEM((384, 2048), BF),
            pltpu.VMEM((256, 2048), F32),
            pltpu.VMEM((128, 128), F32),
            pltpu.VMEM((16384, 256), BF),
            pltpu.VMEM((256, 2048), BF),
            pltpu.VMEM((4, 2, 2, 128, 2048), BF),
            pltpu.VMEM((4, 2, 2, 32, 2048), BF),
            pltpu.VMEM((256, 2048), F32),
            pltpu.VMEM((256, 2048), BF),
            pltpu.SemaphoreType.DMA((6,)),
            pltpu.SemaphoreType.DMA((96,)),
            pltpu.SemaphoreType.DMA((96,)),
        ],
        compiler_params=pltpu.CompilerParams(
            collective_id=0, has_side_effects=True, vmem_limit_bytes=52 << 20
        ),
        cost_estimate=pl.CostEstimate(flops=7_000_000_000, bytes_accessed=20_000_000, transcendentals=131072),
    )(
        qkv, resid, targets, short_filter, long_filter, skip.reshape(1, -1), out_weight,
        gain.reshape(1, -1), vocab_weight,
    )


def solution(mesh):
    in_specs = (
        P("fsdp", "seq", None),
        P("fsdp", "seq", None),
        P("fsdp", "seq"),
        P(),
        P(),
        P(),
        P("fsdp", None),
        P(),
        P("fsdp", None),
    )
    out_specs = P("fsdp", "seq")
    return jax.shard_map(body, mesh=mesh, in_specs=in_specs, out_specs=out_specs, check_vma=False)
```

```python
import jax
import jax.numpy as jnp
from jax import lax
from jax.experimental import pallas as pl
from jax.experimental.pallas import tpu as pltpu
from jax.sharding import PartitionSpec as P

MESH = pl.DeviceIdType.MESH
BF = jnp.bfloat16
F32 = jnp.float32


def place(x, y, z, c):
    x, y, z = lax.rem(x + 4, 4), lax.rem(y + 4, 4), lax.rem(z + 16, 16)
    return (x * 8 + lax.rem(z, 8), (y * 2 + z // 8) * 2 + c)


def cols(start, size):
    return pl.ds(pl.multiple_of(start, 128), size)


def kernel(
    qkv, resid, targets, taps_in, longs_in, skip_in, ow, gain_in, vw, out,
    raw, ext, prod, query, flips, mats, gated, wbuf, stream, base, taps, longs, skip, gain, wanted,
    local_sem, send_sem, recv_sem,
):
    H = 2048
    s, f = lax.axis_index("seq"), lax.axis_index("fsdp")
    x, zl = s // 8, lax.rem(s, 8)
    y, h, c = f // 4, lax.rem(f // 2, 2), lax.rem(f, 2)
    o = 1 - h
    z = h * 8 + zl
    lo, hi = zl == 0, zl == 7
    edge = jnp.logical_or(lo, hi)
    rank = jnp.where(zl < 5, zl, 7 - zl)
    outward = jnp.where(zl < 5, -1, 1)
    passes = jnp.logical_or(zl < 4, zl > 5)

    def xpeer(d):
        return place(x + d, y, z, c)

    def ypeer(d):
        return place(x, y + d, z, c)

    def back(a, d):
        return lax.rem(a + 4 - d, 4)

    outer, inner = place(x, y, z + outward, c), place(x, y, z - outward, c)
    sibling = (s, f + 1 - 2 * c)
    after, before = (lax.rem(s + 1, 32), f), (lax.rem(s + 31, 32), f)
    around, near = (1, 3, 2), (1, 3)

    barrier = pltpu.get_barrier_semaphore()

    def greet(device):
        pl.semaphore_signal(barrier, inc=1, device_id=device, device_id_type=MESH)

    for d in around:
        greet(xpeer(d))
        greet(ypeer(d))
    for device in (sibling, after, before, outer):
        greet(device)

    @pl.when(passes)
    def _():
        greet(inner)

    loads = []

    def load(src, dst):
        copy = pltpu.make_async_copy(src, dst, local_sem.at[len(loads)])
        copy.start()
        loads.append(copy)
        return copy

    def own(half, strip):
        at = pl.ds(strip * 512 + half * 256, 256)
        return [
            load(ow.at[:, at], wbuf.at[y, h, c, half, strip, 0:128]),
            load(vw.at[:, at], wbuf.at[y, h, c, half, strip, 128:160]),
        ]

    load_own = [copy for half in (1, 0) for strip in range(4) for copy in own(half, strip)]
    load_late = load(qkv.at[0, 112:256, H:], raw.at[128:272, H:])
    load_taps = load(taps_in, taps)
    load_early = load(qkv.at[0, 0:112, H:], raw.at[16:128, H:])
    load_q = load(qkv.at[0, :, :H], raw.at[16:272, :H])
    load_rest = [
        load(longs_in, longs), load(skip_in, skip), load(gain_in, gain), load(targets, wanted), load(resid.at[0], base),
    ]

    count = [0]

    def send(src, device, dst=None, slot=None):
        n = count[0]
        count[0] += 1
        return pltpu.make_async_remote_copy(
            src_ref=src, dst_ref=src if dst is None else dst, send_sem=send_sem.at[n],
            recv_sem=recv_sem.at[n if slot is None else slot], device_id=device, device_id_type=MESH,
        )

    def strip(yy, hh, half, xx):
        return wbuf.at[yy, hh, c, half, xx]

    def whole(yy, hh, half):
        return wbuf.at[yy, hh, c, half]

    def column(hh, half, xx):
        return wbuf.at[:, hh, c, half, xx]

    def half_whole(yy, hh, d):
        return wbuf.at[yy, hh, c, 0, 0:2] if d == 1 else wbuf.at[yy, hh, c, 0, 2:4]

    def half_column(xx, d):
        return wbuf.at[0:2, o, c, 1, xx] if d == 1 else wbuf.at[2:4, o, c, 1, xx]

    def piece(hh, k):
        return wbuf.at[y, hh, c, k // 2, x, pl.ds(k % 2 * 80, 80)]

    cross, onward = [], []
    for k in range(4):
        slot = count[0]
        cross.append(send(piece(h, k), outer, slot=slot))
        onward.append(send(piece(o, k), inner, slot=slot))
    heads = send(qkv.at[0, 240:256], after, dst=raw.at[0:16])
    tails = [send(prod.at[256:384, k], after, dst=prod.at[0:128, k]) for k in (pl.ds(0, 1024), pl.ds(1024, 1024))]
    first = {d: send(strip(y, h, 1, x), ypeer(d)) for d in around}
    second = {(k, d): send(strip(back(y, k), h, 1, x), xpeer(d)) for k in around for d in around}
    direct = {d: send(whole(y, h, 0), ypeer(d)) for d in near}
    relay = {d: send(half_whole(back(y, d), h, d), ypeer(d)) for d in near}
    spread0 = {d: send(strip(y, o, 0, x), xpeer(d)) for d in around}
    spread1 = {d: send(strip(y, o, 1, x), ypeer(d)) for d in around}
    wide0 = {d: send(whole(y, o, 0), ypeer(d)) for d in near}
    wide1 = {d: send(column(o, 1, x), xpeer(d)) for d in near}
    relay0 = {d: send(half_whole(back(y, d), o, d), ypeer(d)) for d in near}
    relay1 = {d: send(half_column(back(x, d), d), xpeer(d)) for d in near}
    mate = send(wbuf.at[y, h, c], sibling)
    mate_direct = {d: send(whole(back(y, d), h, 0), sibling) for d in around}
    mate_second = {d: send(whole(back(y, d), h, 1), sibling) for d in around}
    mate_wide0 = {d: send(whole(back(y, d), o, 0), sibling) for d in (0,) + near}
    mate_wide1 = {d: send(column(o, 1, back(x, d)), sibling) for d in (0,) + near}
    mate_relay0 = {d: send(half_whole(back(y, 2), o, d), sibling) for d in near}
    mate_relay1 = {d: send(half_column(back(x, 2), d), sibling) for d in near}

    for copy in load_own:
        copy.wait()
    pl.semaphore_wait(barrier, 10 + jnp.where(passes, 1, 0))

    @pl.when(edge)
    def _():
        for copy in cross:
            copy.start()

    for d in around:
        first[d].start()
    def conv(col, top, spot):
        ext[spot] = raw[top : top + 144, cols(col, 128)].astype(F32)
        total = jnp.zeros((128, 128), F32)
        for lag in range(7):
            total = total + taps[lag : lag + 1, cols(col, 128)] * ext[spot, 16 - lag : 144 - lag]
        return total

    def product(lane, top, spot):
        k = conv(H + lane, top, spot)
        v = conv(2 * H + lane, top, spot + 1)
        prod[128 + top : 256 + top, cols(lane, 128)] = (k * v).astype(BF)

    load_late.wait()
    load_taps.wait()

    @pl.loop(0, 16)
    def _(j):
        product(j * 128, 128, 0)

    def hand_on(*copies):
        for copy in copies:
            copy.start()

    @pl.when(jnp.logical_or(zl == 3, jnp.logical_or(hi, jnp.logical_not(passes))))
    def _():
        hand_on(heads, tails[0])

    @pl.when(jnp.logical_or(hi, jnp.logical_not(passes)))
    def _():
        hand_on(tails[1])

    for d in near:
        direct[d].start()
    mate.start()

    def cross_over(level):
        @pl.when(rank == level)
        def _():
            for k in range(4):
                onward[k].wait_recv()
                if level < 4:
                    pl.when(passes)(onward[k].start)
                if k % 2:
                    for d in around:
                        (spread0, spread1)[k // 2][d].start()

    cross_over(0)

    @pl.when(lo)
    def _():
        hand_on(heads, *tails)

    for k in around:
        first[k].wait_recv()
        for d in around:
            second[k, d].start()

    cross_over(1)

    @pl.when(rank == 1)
    def _():
        hand_on(heads, *tails)

    rows = lax.broadcasted_iota(jnp.int32, (128, 128), 0)
    lanes = lax.broadcasted_iota(jnp.int32, (128, 128), 1)
    turn = jnp.where(lax.rem(rows + lanes, 128) == 0, 1.0, 0.0).astype(BF)
    load_rest[0].wait()
    flips[...] = jnp.dot(longs[...], turn, preferred_element_type=F32)

    @pl.loop(0, 16)
    def _(j):
        for k in range(8):
            g = j * 8 + k
            spin = pltpu.roll(jnp.broadcast_to(flips[pl.ds(g, 1), :], (128, 128)), 0, 1, stride=1, stride_axis=0)
            at = pl.ds(pl.multiple_of(g * 128, 128), 128)
            mats[at, 0:128] = jnp.where(lanes > rows, spin, 0.0).astype(BF)
            mats[at, 128:256] = jnp.where(lanes > rows, 0.0, spin).astype(BF)

    cross_over(2)

    @pl.when(zl == 2)
    def _():
        hand_on(heads, *tails)

    cross_over(3)

    @pl.when(zl == 3)
    def _():
        hand_on(tails[1])

    for d in near:
        direct[d].wait_recv()
        relay[d].start()
    cross_over(4)
    for d in near:
        mate_direct[d].start()
    for k in around:
        for d in around:
            second[k, d].wait_recv()
        mate_second[k].start()
    for d in around:
        spread0[d].wait_recv()
    for d in near:
        wide0[d].start()
    for d in around:
        spread1[d].wait_recv()
    for d in near:
        wide1[d].start()
    mate_wide0[0].start()
    mate_wide1[0].start()
    for d in near:
        relay[d].wait_recv()
    mate_direct[2].start()

    def pass_wide():
        for d in near:
            wide0[d].wait_recv()
            relay0[d].start()
            wide1[d].wait_recv()
            relay1[d].start()
        for d in near:
            mate_wide0[d].start()
            mate_wide1[d].start()

    hurry = jnp.logical_or(zl == 0, zl == 4)
    pl.when(hurry)(pass_wide)
    load_early.wait()
    load_q.wait()
    for copy in load_rest[1:]:
        copy.wait()
    heads.wait_recv()

    @pl.when(s == 0)
    def _():
        raw[0:16] = jnp.zeros((16, 3 * H), BF)

    @pl.loop(0, 16)
    def _(j):
        lane = j * 128
        product(lane, 0, 0)
        query[0:128, cols(lane, 128)] = conv(lane, 0, 2)
        query[128:256, cols(lane, 128)] = conv(lane, 128, 3)

    for copy in tails:
        copy.wait_recv()

    @pl.when(s == 0)
    def _():
        prod[0:128] = jnp.zeros((128, H), BF)

    group = lax.broadcasted_iota(jnp.int32, (128, 128), 1) // 16

    @pl.loop(0, 16)
    def _(j):
        lane = cols(j * 128, 128)
        pair = jnp.concatenate([prod[0:256, lane], prod[128:384, lane]], axis=1)
        spans = jnp.dot(mats[pl.ds(pl.multiple_of(j * 1024, 1024), 1024), :], pair, preferred_element_type=F32)
        for b in (0, 1):
            wave = spans[0:128, b * 128 : b * 128 + 128]
            for g in range(1, 8):
                wave = jnp.where(group == g, spans[g * 128 : g * 128 + 128, b * 128 : b * 128 + 128], wave)
            at = slice(b * 128, b * 128 + 128)
            wave = wave + skip[:, lane] * prod[b * 128 + 128 : b * 128 + 256, lane].astype(F32)
            gated[at, lane] = (query[at, lane] * wave).astype(BF)

    def project(hh, half, xx):
        left = jnp.concatenate([gated[:, cols((yy * 2 + hh) * 256, 256)] for yy in range(4)], axis=1)
        right = jnp.concatenate([wbuf[yy, hh, :, half, xx, 0:128, :].reshape(256, 256) for yy in range(4)], axis=0)
        return jnp.dot(left, right, preferred_element_type=F32)

    pl.when(jnp.logical_not(hurry))(pass_wide)
    mate.wait_recv()
    for d in around:
        mate_direct[d].wait_recv()
    for d in around:
        mate_second[d].wait_recv()

    @pl.loop(0, 8)
    def _(n):
        half, xx = n // 4, lax.rem(n, 4)
        at = cols(xx * 512 + half * 256, 256)
        stream[:, at] = base[:, at].astype(F32) + project(h, half, xx)

    for d in near:
        relay0[d].wait_recv()
        mate_relay0[d].start()
        relay1[d].wait_recv()
        mate_relay1[d].start()
    for group_of in (mate_wide0, mate_wide1, mate_relay0, mate_relay1):
        for copy in group_of.values():
            copy.wait_recv()

    def close(n, squares):
        half, xx = n // 4, lax.rem(n, 4)
        at = cols(xx * 512 + half * 256, 256)
        total = stream[:, at] + project(o, half, xx)
        stream[:, at] = total
        return squares + total[:, :128] * total[:, :128] + total[:, 128:] * total[:, 128:]

    squares = lax.fori_loop(0, 8, close, jnp.zeros((256, 128), F32))
    scale = lax.rsqrt(jnp.sum(squares, axis=1, keepdims=True) / 2048.0 + 1e-05)

    @pl.loop(0, 8)
    def _(n):
        at = cols(n * 256, 256)
        gated[:, at] = (stream[:, at] * scale * gain[:, at]).astype(BF)

    words = jnp.concatenate(
        [wbuf[:, :, :, n % 2, n // 2, 128:160, :].reshape(512, 256) for n in range(8)], axis=1
    )
    logits = lax.dot_general(words, gated[...], (((1,), (1,)), ((), ())), preferred_element_type=F32)
    top = jnp.max(logits, axis=0, keepdims=True)
    total = top + jnp.log(jnp.sum(jnp.exp(logits - top), axis=0, keepdims=True))
    entry = lax.broadcasted_iota(jnp.int32, (512, 256), 0)
    out[...] = jnp.sum(jnp.where(entry == wanted[...], logits, 0.0), axis=0, keepdims=True) - total

    @pl.when(edge)
    def _():
        for copy in cross:
            copy.wait_send()

    @pl.when(passes)
    def _():
        for copy in onward:
            copy.wait_send()

    for copy in (heads, *tails, mate):
        copy.wait_send()
    for group_of in (
        first, second, direct, relay, spread0, spread1, wide0, wide1, relay0, relay1, mate_direct, mate_second, mate_wide0, mate_wide1,
        mate_relay0, mate_relay1,
    ):
        for copy in group_of.values():
            copy.wait_send()


def body(qkv, resid, targets, short_filter, long_filter, skip, out_weight, gain, vocab_weight):
    vmem = pl.BlockSpec(memory_space=pltpu.VMEM)
    hbm = pl.BlockSpec(memory_space=pltpu.HBM)
    return pl.pallas_call(
        kernel,
        name="hyena_block",
        out_shape=jax.ShapeDtypeStruct((1, 256), F32),
        in_specs=[hbm] * 9,
        out_specs=vmem,
        scratch_shapes=[
            pltpu.VMEM((272, 6144), BF),
            pltpu.VMEM((4, 144, 128), F32),
            pltpu.VMEM((384, 2048), BF),
            pltpu.VMEM((256, 2048), F32),
            pltpu.VMEM((128, 128), F32),
            pltpu.VMEM((16384, 256), BF),
            pltpu.VMEM((256, 2048), BF),
            pltpu.VMEM((4, 2, 2, 2, 4, 160, 256), BF),
            pltpu.VMEM((256, 2048), F32),
            pltpu.VMEM((256, 2048), BF),
            pltpu.VMEM((7, 6144), F32),
            pltpu.VMEM((128, 128), BF),
            pltpu.VMEM((1, 2048), F32),
            pltpu.VMEM((1, 2048), F32),
            pltpu.VMEM((1, 256), jnp.int32),
            pltpu.SemaphoreType.DMA((32,)),
            pltpu.SemaphoreType.DMA((72,)),
            pltpu.SemaphoreType.DMA((72,)),
        ],
        compiler_params=pltpu.CompilerParams(
            collective_id=0, has_side_effects=True, vmem_limit_bytes=60 << 20
        ),
        cost_estimate=pl.CostEstimate(flops=7_000_000_000, bytes_accessed=20_000_000, transcendentals=131072),
    )(
        qkv, resid, targets, short_filter, long_filter, skip.reshape(1, -1), out_weight,
        gain.reshape(1, -1), vocab_weight,
    )


def solution(mesh):
    in_specs = (
        P("fsdp", "seq", None),
        P("fsdp", "seq", None),
        P("fsdp", "seq"),
        P(),
        P(),
        P(),
        P("fsdp", None),
        P(),
        P("fsdp", None),
    )
    out_specs = P("fsdp", "seq")
    return jax.shard_map(body, mesh=mesh, in_specs=in_specs, out_specs=out_specs, check_vma=False)
```

```python
import jax
import jax.numpy as jnp
from jax import lax
from jax.experimental import pallas as pl
from jax.experimental.pallas import tpu as pltpu
from jax.sharding import PartitionSpec as P

MESH = pl.DeviceIdType.MESH
BF = jnp.bfloat16
F32 = jnp.float32


def place(x, y, z, c):
    x, y, z = lax.rem(x + 4, 4), lax.rem(y + 4, 4), lax.rem(z + 16, 16)
    return (x * 8 + lax.rem(z, 8), (y * 2 + z // 8) * 2 + c)


def cols(start, size):
    return pl.ds(pl.multiple_of(start, 128), size)


def kernel(
    qkv, resid, targets, taps_in, longs_in, skip_in, ow, gain_in, vw, out,
    raw, ext, pack, prod, ferry, query, flips, mats, gated, wbuf, stream, base, taps, longs, skip, gain, wanted,
    local_sem, send_sem, recv_sem,
):
    H = 2048
    s, f = lax.axis_index("seq"), lax.axis_index("fsdp")
    x, zl = s // 8, lax.rem(s, 8)
    y, h, c = f // 4, lax.rem(f // 2, 2), lax.rem(f, 2)
    o = 1 - h
    z = h * 8 + zl
    lo, hi = zl == 0, zl == 7
    edge = jnp.logical_or(lo, hi)
    rank = jnp.where(zl < 5, zl, 7 - zl)
    outward = jnp.where(zl < 5, -1, 1)
    passes = jnp.logical_or(zl < 4, zl > 5)

    def xpeer(d):
        return place(x + d, y, z, c)

    def ypeer(d):
        return place(x, y + d, z, c)

    def back(a, d):
        return lax.rem(a + 4 - d, 4)

    outer, inner = place(x, y, z + outward, c), place(x, y, z - outward, c)
    sibling = (s, f + 1 - 2 * c)
    after, before = (lax.rem(s + 1, 32), f), (lax.rem(s + 31, 32), f)
    around, near = (1, 3, 2), (1, 3)

    barrier = pltpu.get_barrier_semaphore()

    def greet(device):
        pl.semaphore_signal(barrier, inc=1, device_id=device, device_id_type=MESH)

    for d in around:
        greet(xpeer(d))
        greet(ypeer(d))
    for device in (sibling, after, before, outer):
        greet(device)

    @pl.when(passes)
    def _():
        greet(inner)

    far = place(x, y, jnp.where(lo, z + 7, z - 7), c)

    @pl.when(edge)
    def _():
        greet(far)

    loads = []

    def load(src, dst):
        copy = pltpu.make_async_copy(src, dst, local_sem.at[len(loads)])
        copy.start()
        loads.append(copy)
        return copy

    def own(half, strip):
        at = pl.ds(strip * 512 + half * 256, 256)
        return [
            load(ow.at[:, at], wbuf.at[y, h, c, half, strip, 0:128]),
            load(vw.at[:, at], wbuf.at[y, h, c, half, strip, 128:160]),
        ]

    load_own = [copy for half in (1, 0) for strip in range(4) for copy in own(half, strip)]
    load_late = load(qkv.at[0, 112:256, H:], raw.at[128:272, H:])
    load_taps = load(taps_in, taps)
    load_early = load(qkv.at[0, 0:112, H:], raw.at[16:128, H:])
    load_q = load(qkv.at[0, :, :H], raw.at[16:272, :H])
    load_rest = [
        load(longs_in, longs), load(skip_in, skip), load(gain_in, gain), load(targets, wanted), load(resid.at[0], base),
    ]

    count = [0]

    def send(src, device, dst=None, slot=None):
        n = count[0]
        count[0] += 1
        return pltpu.make_async_remote_copy(
            src_ref=src, dst_ref=src if dst is None else dst, send_sem=send_sem.at[n],
            recv_sem=recv_sem.at[n if slot is None else slot], device_id=device, device_id_type=MESH,
        )

    def strip(yy, hh, half, xx):
        return wbuf.at[yy, hh, c, half, xx]

    def whole(yy, hh, half):
        return wbuf.at[yy, hh, c, half]

    def column(hh, half, xx):
        return wbuf.at[:, hh, c, half, xx]

    def half_whole(yy, hh, d):
        return wbuf.at[yy, hh, c, 0, 0:2] if d == 1 else wbuf.at[yy, hh, c, 0, 2:4]

    def half_column(xx, d):
        return wbuf.at[0:2, o, c, 1, xx] if d == 1 else wbuf.at[2:4, o, c, 1, xx]

    def piece(hh, k):
        return wbuf.at[y, hh, c, k // 2, x, pl.ds(k % 2 * 80, 80)]

    cross, onward = [], []
    for k in range(4):
        slot = count[0]
        cross.append(send(piece(h, k), outer, slot=slot))
        onward.append(send(piece(o, k), inner, slot=slot))
    heads = send(pack.at[0], after, dst=pack.at[1])
    tails = [send(prod.at[256:384, k], after, dst=prod.at[0:128, k]) for k in (pl.ds(0, 1024), pl.ds(1024, 1024))]
    ferry_out = send(prod.at[256:384, 1024:], xpeer(1), dst=ferry)
    ferry_on = send(ferry, far, dst=prod.at[0:128, 1024:], slot=count[0] - 2)
    first = {d: send(strip(y, h, 1, x), ypeer(d)) for d in around}
    second = {(k, d): send(strip(back(y, k), h, 1, x), xpeer(d)) for k in around for d in near}
    second_on = {
        (k, d): send(strip(back(y, k), h, 1, back(x, d)), xpeer(d)) for k, d in ((1, 1), (3, 3))
    }
    for d in near:
        second_on[2, d] = send(wbuf.at[back(y, 2), h, c, 1, back(x, d), pl.ds(d // 2 * 80, 80)], xpeer(d))
    direct = {d: send(whole(y, h, 0), ypeer(d)) for d in near}
    relay = {d: send(half_whole(back(y, d), h, d), ypeer(d)) for d in near}
    spread0 = {d: send(strip(y, o, 0, x), xpeer(d)) for d in around}
    spread1 = {d: send(strip(y, o, 1, x), ypeer(d)) for d in around}
    wide0 = {d: send(whole(y, o, 0), ypeer(d)) for d in near}
    wide1 = {d: send(column(o, 1, x), xpeer(d)) for d in near}
    relay0 = {d: send(half_whole(back(y, d), o, d), ypeer(d)) for d in near}
    relay1 = {d: send(half_column(back(x, d), d), xpeer(d)) for d in near}
    mate = send(wbuf.at[y, h, c], sibling)
    mate_direct = {d: send(whole(back(y, d), h, 0), sibling) for d in around}
    mate_second = {d: send(whole(back(y, d), h, 1), sibling) for d in around}
    mate_wide0 = {d: send(whole(back(y, d), o, 0), sibling) for d in (0,) + near}
    mate_wide1 = {d: send(column(o, 1, back(x, d)), sibling) for d in (0,) + near}
    mate_relay0 = {d: send(half_whole(back(y, 2), o, d), sibling) for d in near}
    mate_relay1 = {d: send(half_column(back(x, 2), d), sibling) for d in near}

    for copy in load_own:
        copy.wait()
    pl.semaphore_wait(barrier, 10 + jnp.where(passes, 1, 0) + jnp.where(edge, 1, 0))

    @pl.when(edge)
    def _():
        for copy in cross:
            copy.start()

    for d in around:
        first[d].start()
    def conv(col, top, spot):
        ext[spot] = raw[top : top + 144, cols(col, 128)].astype(F32)
        total = jnp.zeros((128, 128), F32)
        for lag in range(7):
            total = total + taps[lag : lag + 1, cols(col, 128)] * ext[spot, 16 - lag : 144 - lag]
        return total

    def product(lane, top, spot):
        k = conv(H + lane, top, spot)
        v = conv(2 * H + lane, top, spot + 1)
        prod[128 + top : 256 + top, cols(lane, 128)] = (k * v).astype(BF)

    load_late.wait()
    load_taps.wait()
    load_q.wait()
    last = raw[256:272].astype(F32)[8:16]
    pack[0] = jnp.concatenate([last[:, :3072], last[:, 3072:]], axis=0).astype(BF)

    @pl.loop(0, 16)
    def _(j):
        product(j * 128, 128, 0)

    def hand_on(*copies):
        for copy in copies:
            copy.start()

    @pl.when(hi)
    def _():
        hand_on(ferry_out)

    @pl.when(jnp.logical_or(zl == 3, jnp.logical_not(passes)))
    def _():
        hand_on(heads, tails[0])

    @pl.when(jnp.logical_not(passes))
    def _():
        hand_on(tails[1])

    for d in near:
        direct[d].start()
    mate.start()

    def cross_over(level):
        @pl.when(rank == level)
        def _():
            for k in range(4):
                onward[k].wait_recv()
                if level < 4:
                    pl.when(passes)(onward[k].start)
                if k % 2:
                    for d in around:
                        (spread0, spread1)[k // 2][d].start()

    cross_over(0)

    @pl.when(lo)
    def _():
        hand_on(heads, *tails)

    for k in around:
        first[k].wait_recv()
        for d in near:
            second[k, d].start()

    cross_over(1)

    @pl.when(rank == 1)
    def _():
        hand_on(heads, *tails)

    rows = lax.broadcasted_iota(jnp.int32, (128, 128), 0)
    lanes = lax.broadcasted_iota(jnp.int32, (128, 128), 1)
    turn = jnp.where(lax.rem(rows + lanes, 128) == 0, 1.0, 0.0).astype(BF)
    load_rest[0].wait()
    flips[...] = jnp.dot(longs[...], turn, preferred_element_type=F32)

    @pl.loop(0, 16)
    def _(j):
        for k in range(8):
            g = j * 8 + k
            spin = pltpu.roll(jnp.broadcast_to(flips[pl.ds(g, 1), :], (128, 128)), 0, 1, stride=1, stride_axis=0)
            at = pl.ds(pl.multiple_of(g * 128, 128), 128)
            mats[at, 0:128] = jnp.where(lanes > rows, spin, 0.0).astype(BF)
            mats[at, 128:256] = jnp.where(lanes > rows, 0.0, spin).astype(BF)

    cross_over(2)

    @pl.when(zl == 2)
    def _():
        hand_on(heads, *tails)

    cross_over(3)

    @pl.when(zl == 3)
    def _():
        hand_on(tails[1])

    cross_over(4)
    for copy in second.values():
        copy.wait_recv()
    for copy in second_on.values():
        copy.start()

    @pl.when(hi)
    def _():
        hand_on(heads, tails[0])
        ferry_out.wait_recv()
        ferry_on.start()

    for d in near:
        direct[d].wait_recv()
        relay[d].start()
    for d in near:
        mate_direct[d].start()
    for copy in second_on.values():
        copy.wait_recv()
    for d in around:
        mate_second[d].start()
    for d in around:
        spread0[d].wait_recv()
    for d in near:
        wide0[d].start()
    for d in around:
        spread1[d].wait_recv()
    wide1[3].start()
    pl.when(jnp.logical_not(lo))(wide1[1].start)
    mate_wide0[0].start()
    mate_wide1[0].start()
    for d in near:
        relay[d].wait_recv()
    mate_direct[2].start()

    def pass_wide():
        for d in near:
            wide0[d].wait_recv()
            relay0[d].start()
            wide1[d].wait_recv()
            relay1[d].start()
        for d in near:
            mate_wide0[d].start()
            mate_wide1[d].start()

    load_early.wait()
    for copy in load_rest[1:]:
        copy.wait()
    heads.wait_recv()
    got = jnp.where(s == 0, 0.0, pack[1].astype(F32))
    raw[0:16, :3072] = jnp.concatenate([got[0:8], got[0:8]], axis=0).astype(BF)
    raw[0:16, 3072:] = jnp.concatenate([got[8:16], got[8:16]], axis=0).astype(BF)

    @pl.when(lo)
    def _():
        for copy in tails:
            copy.wait_recv()
        wide1[1].start()

    @pl.loop(0, 16)
    def _(j):
        lane = j * 128
        product(lane, 0, 0)
        query[0:128, cols(lane, 128)] = conv(lane, 0, 2)
        query[128:256, cols(lane, 128)] = conv(lane, 128, 3)

    @pl.when(jnp.logical_not(lo))
    def _():
        for copy in tails:
            copy.wait_recv()

    @pl.when(s == 0)
    def _():
        prod[0:128] = jnp.zeros((128, H), BF)

    group = lax.broadcasted_iota(jnp.int32, (128, 128), 1) // 16

    @pl.loop(0, 16)
    def _(j):
        lane = cols(j * 128, 128)
        pair = jnp.concatenate([prod[0:256, lane], prod[128:384, lane]], axis=1)
        spans = jnp.dot(mats[pl.ds(pl.multiple_of(j * 1024, 1024), 1024), :], pair, preferred_element_type=F32)
        for b in (0, 1):
            wave = spans[0:128, b * 128 : b * 128 + 128]
            for g in range(1, 8):
                wave = jnp.where(group == g, spans[g * 128 : g * 128 + 128, b * 128 : b * 128 + 128], wave)
            at = slice(b * 128, b * 128 + 128)
            wave = wave + skip[:, lane] * prod[b * 128 + 128 : b * 128 + 256, lane].astype(F32)
            gated[at, lane] = (query[at, lane] * wave).astype(BF)

    def tile(half, xx):
        return cols(xx * 512 + half * 256, 256)

    def project(hh, half, xx, blocks):
        left = jnp.concatenate([gated[:, cols((yy * 2 + hh) * 256, 256)] for yy in blocks], axis=1)
        right = jnp.concatenate([wbuf[yy, hh, :, half, xx, 0:128, :].reshape(256, 256) for yy in blocks], axis=0)
        return jnp.dot(left, right, preferred_element_type=F32)

    def gather_in(half, xx, blocks):
        at = tile(half, xx)
        stream[:, at] = stream[:, at] + project(o, half, xx, blocks)

    pass_wide()
    mate.wait_recv()
    for d in around:
        mate_direct[d].wait_recv()
    for d in around:
        mate_second[d].wait_recv()

    @pl.loop(0, 8)
    def _(n):
        half, xx = n // 4, lax.rem(n, 4)
        at = tile(half, xx)
        stream[:, at] = base[:, at].astype(F32) + project(h, half, xx, range(4))

    for group_of in (mate_wide0, mate_wide1):
        for copy in group_of.values():
            copy.wait_recv()

    @pl.loop(0, 3)
    def _(n):
        gather_in(1, lax.rem(x + 3 + n, 4), range(4))

    @pl.loop(0, 4)
    def _(n):
        gather_in(0, n, [lax.rem(y + 3 + k, 4) for k in range(3)])

    for d in near:
        relay0[d].wait_recv()
        mate_relay0[d].start()
        relay1[d].wait_recv()
        mate_relay1[d].start()
    for group_of in (mate_relay0, mate_relay1):
        for copy in group_of.values():
            copy.wait_recv()

    gather_in(1, lax.rem(x + 2, 4), range(4))

    def close(n, squares):
        gather_in(0, n, [lax.rem(y + 2, 4)])
        for half in (0, 1):
            total = stream[:, tile(half, n)]
            squares = squares + total[:, :128] * total[:, :128] + total[:, 128:] * total[:, 128:]
        return squares

    squares = lax.fori_loop(0, 4, close, jnp.zeros((256, 128), F32))
    scale = lax.rsqrt(jnp.sum(squares, axis=1, keepdims=True) / 2048.0 + 1e-05)

    @pl.loop(0, 8)
    def _(n):
        at = cols(n * 256, 256)
        gated[:, at] = (stream[:, at] * scale * gain[:, at]).astype(BF)

    words = jnp.concatenate(
        [wbuf[:, :, :, n % 2, n // 2, 128:160, :].reshape(512, 256) for n in range(8)], axis=1
    )
    logits = lax.dot_general(words, gated[...], (((1,), (1,)), ((), ())), preferred_element_type=F32)
    top = jnp.max(logits, axis=0, keepdims=True)
    total = top + jnp.log(jnp.sum(jnp.exp(logits - top), axis=0, keepdims=True))
    entry = lax.broadcasted_iota(jnp.int32, (512, 256), 0)
    out[...] = jnp.sum(jnp.where(entry == wanted[...], logits, 0.0), axis=0, keepdims=True) - total

    @pl.when(edge)
    def _():
        for copy in cross:
            copy.wait_send()

    @pl.when(passes)
    def _():
        for copy in onward:
            copy.wait_send()

    @pl.when(hi)
    def _():
        ferry_out.wait_send()
        ferry_on.wait_send()

    @pl.when(jnp.logical_not(hi))
    def _():
        tails[1].wait_send()

    for copy in (heads, tails[0], mate):
        copy.wait_send()
    for group_of in (
        first, second, second_on, direct, relay, spread0, spread1, wide0, wide1, relay0, relay1, mate_direct, mate_second, mate_wide0, mate_wide1,
        mate_relay0, mate_relay1,
    ):
        for copy in group_of.values():
            copy.wait_send()


def body(qkv, resid, targets, short_filter, long_filter, skip, out_weight, gain, vocab_weight):
    vmem = pl.BlockSpec(memory_space=pltpu.VMEM)
    hbm = pl.BlockSpec(memory_space=pltpu.HBM)
    return pl.pallas_call(
        kernel,
        name="hyena_block",
        out_shape=jax.ShapeDtypeStruct((1, 256), F32),
        in_specs=[hbm] * 9,
        out_specs=vmem,
        scratch_shapes=[
            pltpu.VMEM((272, 6144), BF),
            pltpu.VMEM((4, 144, 128), F32),
            pltpu.VMEM((2, 16, 3072), BF),
            pltpu.VMEM((384, 2048), BF),
            pltpu.VMEM((128, 1024), BF),
            pltpu.VMEM((256, 2048), F32),
            pltpu.VMEM((128, 128), F32),
            pltpu.VMEM((16384, 256), BF),
            pltpu.VMEM((256, 2048), BF),
            pltpu.VMEM((4, 2, 2, 2, 4, 160, 256), BF),
            pltpu.VMEM((256, 2048), F32),
            pltpu.VMEM((256, 2048), BF),
            pltpu.VMEM((7, 6144), F32),
            pltpu.VMEM((128, 128), BF),
            pltpu.VMEM((1, 2048), F32),
            pltpu.VMEM((1, 2048), F32),
            pltpu.VMEM((1, 256), jnp.int32),
            pltpu.SemaphoreType.DMA((32,)),
            pltpu.SemaphoreType.DMA((72,)),
            pltpu.SemaphoreType.DMA((72,)),
        ],
        compiler_params=pltpu.CompilerParams(
            collective_id=0, has_side_effects=True, vmem_limit_bytes=60 << 20
        ),
        cost_estimate=pl.CostEstimate(flops=7_000_000_000, bytes_accessed=20_000_000, transcendentals=131072),
    )(
        qkv, resid, targets, short_filter, long_filter, skip.reshape(1, -1), out_weight,
        gain.reshape(1, -1), vocab_weight,
    )


def solution(mesh):
    in_specs = (
        P("fsdp", "seq", None),
        P("fsdp", "seq", None),
        P("fsdp", "seq"),
        P(),
        P(),
        P(),
        P("fsdp", None),
        P(),
        P("fsdp", None),
    )
    out_specs = P("fsdp", "seq")
    return jax.shard_map(body, mesh=mesh, in_specs=in_specs, out_specs=out_specs, check_vma=False)
```

```python
import jax
import jax.numpy as jnp
from jax import lax
from jax.experimental import pallas as pl
from jax.experimental.pallas import tpu as pltpu
from jax.sharding import PartitionSpec as P

MESH = pl.DeviceIdType.MESH
BF = jnp.bfloat16
F32 = jnp.float32


def place(x, y, z, c):
    x, y, z = lax.rem(x + 4, 4), lax.rem(y + 4, 4), lax.rem(z + 16, 16)
    return (x * 8 + lax.rem(z, 8), (y * 2 + z // 8) * 2 + c)


def cols(start, size):
    return pl.ds(pl.multiple_of(start, 128), size)


def kernel(
    qkv, resid, targets, taps_in, longs_in, skip_in, ow, gain_in, vw, out,
    raw, ext, pack, prod, ferry, query, flips, mats, gated, wbuf, stream, base, taps, longs, skip, gain, wanted,
    local_sem, send_sem, recv_sem,
):
    H = 2048
    s, f = lax.axis_index("seq"), lax.axis_index("fsdp")
    x, zl = s // 8, lax.rem(s, 8)
    y, h, c = f // 4, lax.rem(f // 2, 2), lax.rem(f, 2)
    o = 1 - h
    z = h * 8 + zl
    lo, hi = zl == 0, zl == 7
    edge = jnp.logical_or(lo, hi)
    rank = jnp.where(zl < 5, zl, 7 - zl)
    outward = jnp.where(zl < 5, -1, 1)
    passes = jnp.logical_or(zl < 4, zl > 5)

    def xpeer(d):
        return place(x + d, y, z, c)

    def ypeer(d):
        return place(x, y + d, z, c)

    def back(a, d):
        return lax.rem(a + 4 - d, 4)

    outer, inner = place(x, y, z + outward, c), place(x, y, z - outward, c)
    sibling = (s, f + 1 - 2 * c)
    after, before = (lax.rem(s + 1, 32), f), (lax.rem(s + 31, 32), f)
    around, near = (1, 3, 2), (1, 3)

    barrier = pltpu.get_barrier_semaphore()

    def greet(device):
        pl.semaphore_signal(barrier, inc=1, device_id=device, device_id_type=MESH)

    for d in around:
        greet(xpeer(d))
        greet(ypeer(d))
    for device in (sibling, after, before, outer):
        greet(device)

    @pl.when(passes)
    def _():
        greet(inner)

    far = place(x, y, jnp.where(lo, z + 7, z - 7), c)

    @pl.when(edge)
    def _():
        greet(far)

    loads = []

    def load(src, dst):
        copy = pltpu.make_async_copy(src, dst, local_sem.at[len(loads)])
        copy.start()
        loads.append(copy)
        return copy

    def own(half, strip):
        at = pl.ds(strip * 512 + half * 256, 256)
        return [
            load(ow.at[:, at], wbuf.at[y, h, c, half, strip, 0:128]),
            load(vw.at[:, at], wbuf.at[y, h, c, half, strip, 128:160]),
        ]

    load_own = [copy for half in (1, 0) for strip in range(4) for copy in own(half, strip)]
    load_late = load(qkv.at[0, 112:256, H:], raw.at[128:272, H:])
    load_taps = load(taps_in, taps)
    load_early = load(qkv.at[0, 0:112, H:], raw.at[16:128, H:])
    load_q = load(qkv.at[0, :, :H], raw.at[16:272, :H])
    load_rest = [
        load(longs_in, longs), load(skip_in, skip), load(gain_in, gain), load(targets, wanted), load(resid.at[0], base),
    ]

    count = [0]

    def send(src, device, dst=None, slot=None):
        n = count[0]
        count[0] += 1
        return pltpu.make_async_remote_copy(
            src_ref=src, dst_ref=src if dst is None else dst, send_sem=send_sem.at[n],
            recv_sem=recv_sem.at[n if slot is None else slot], device_id=device, device_id_type=MESH,
        )

    def strip(yy, hh, half, xx):
        return wbuf.at[yy, hh, c, half, xx]

    def whole(yy, hh, half):
        return wbuf.at[yy, hh, c, half]

    def column(hh, half, xx):
        return wbuf.at[:, hh, c, half, xx]

    def half_whole(yy, hh, d):
        return wbuf.at[yy, hh, c, 0, 0:2] if d == 1 else wbuf.at[yy, hh, c, 0, 2:4]

    def half_column(xx, d):
        return wbuf.at[0:2, o, c, 1, xx] if d == 1 else wbuf.at[2:4, o, c, 1, xx]

    def piece(hh, k):
        return wbuf.at[y, hh, c, k // 2, x, pl.ds(k % 2 * 80, 80)]

    cross, onward = [], []
    for k in range(4):
        slot = count[0]
        cross.append(send(piece(h, k), outer, slot=slot))
        onward.append(send(piece(o, k), inner, slot=slot))
    heads = send(pack.at[0], after, dst=pack.at[1])
    tails, ferry_out, ferry_on = [], [], []
    for k in (0, 1):
        at, slot = pl.ds(k * 1024, 1024), count[0]
        tails.append(send(prod.at[256:384, at], after, dst=prod.at[0:128, at]))
        ferry_out.append(send(prod.at[256:384, at], xpeer(1), dst=ferry.at[k]))
        ferry_on.append(send(ferry.at[k], far, dst=prod.at[0:128, at], slot=slot))
    first = {d: send(strip(y, h, 1, x), ypeer(d)) for d in around}
    second = {(k, d): send(strip(back(y, k), h, 1, x), xpeer(d)) for k in around for d in near}
    second_on = {
        (k, d): send(strip(back(y, k), h, 1, back(x, d)), xpeer(d)) for k, d in ((1, 1), (3, 3))
    }
    for d in near:
        second_on[2, d] = send(wbuf.at[back(y, 2), h, c, 1, back(x, d), pl.ds(d // 2 * 80, 80)], xpeer(d))
    direct = {d: send(whole(y, h, 0), ypeer(d)) for d in near}
    relay = {d: send(half_whole(back(y, d), h, d), ypeer(d)) for d in near}
    spread0 = {d: send(strip(y, o, 0, x), xpeer(d)) for d in around}
    spread1 = {d: send(strip(y, o, 1, x), ypeer(d)) for d in around}
    wide0 = {d: send(whole(y, o, 0), ypeer(d)) for d in near}
    wide1 = {d: send(column(o, 1, x), xpeer(d)) for d in near}
    relay0 = {d: send(half_whole(back(y, d), o, d), ypeer(d)) for d in near}
    relay1 = {d: send(half_column(back(x, d), d), xpeer(d)) for d in near}
    mate = send(wbuf.at[y, h, c], sibling)
    mate_direct = {d: send(whole(back(y, d), h, 0), sibling) for d in around}
    mate_second = {d: send(whole(back(y, d), h, 1), sibling) for d in around}
    mate_wide0 = {d: send(whole(back(y, d), o, 0), sibling) for d in (0,) + near}
    mate_wide1 = {d: send(column(o, 1, back(x, d)), sibling) for d in (0,) + near}
    mate_relay0 = {d: send(half_whole(back(y, 2), o, d), sibling) for d in near}
    mate_relay1 = {d: send(half_column(back(x, 2), d), sibling) for d in near}

    for copy in load_own:
        copy.wait()
    pl.semaphore_wait(barrier, 10 + jnp.where(passes, 1, 0) + jnp.where(edge, 1, 0))

    @pl.when(edge)
    def _():
        for copy in cross:
            copy.start()

    for d in around:
        first[d].start()
    def conv(col, top, spot):
        ext[spot] = raw[top : top + 144, cols(col, 128)].astype(F32)
        total = jnp.zeros((128, 128), F32)
        for lag in range(7):
            total = total + taps[lag : lag + 1, cols(col, 128)] * ext[spot, 16 - lag : 144 - lag]
        return total

    def product(lane, top, spot):
        k = conv(H + lane, top, spot)
        v = conv(2 * H + lane, top, spot + 1)
        prod[128 + top : 256 + top, cols(lane, 128)] = (k * v).astype(BF)

    load_late.wait()
    load_taps.wait()
    load_q.wait()
    last = raw[256:272].astype(F32)[8:16]
    pack[0] = jnp.concatenate([last[:, :3072], last[:, 3072:]], axis=0).astype(BF)

    @pl.loop(0, 16)
    def _(j):
        product(j * 128, 128, 0)

    def hand_on(*copies):
        for copy in copies:
            copy.start()

    @pl.when(hi)
    def _():
        hand_on(*ferry_out)

    @pl.when(jnp.logical_or(zl == 3, jnp.logical_not(passes)))
    def _():
        hand_on(heads, tails[0])

    @pl.when(jnp.logical_not(passes))
    def _():
        hand_on(tails[1])

    for d in near:
        direct[d].start()
    mate.start()

    def cross_over(level):
        @pl.when(rank == level)
        def _():
            for k in range(4):
                onward[k].wait_recv()
                if level < 4:
                    pl.when(passes)(onward[k].start)
                if k % 2:
                    for d in around:
                        (spread0, spread1)[k // 2][d].start()

    cross_over(0)

    @pl.when(lo)
    def _():
        hand_on(heads, *tails)

    for k in around:
        first[k].wait_recv()
        for d in near:
            second[k, d].start()

    cross_over(1)

    @pl.when(rank == 1)
    def _():
        hand_on(heads, *tails)

    rows = lax.broadcasted_iota(jnp.int32, (128, 128), 0)
    lanes = lax.broadcasted_iota(jnp.int32, (128, 128), 1)
    turn = jnp.where(lax.rem(rows + lanes, 128) == 0, 1.0, 0.0).astype(BF)
    load_rest[0].wait()
    flips[...] = jnp.dot(longs[...], turn, preferred_element_type=F32)

    @pl.loop(0, 16)
    def _(j):
        for k in range(8):
            g = j * 8 + k
            spin = pltpu.roll(jnp.broadcast_to(flips[pl.ds(g, 1), :], (128, 128)), 0, 1, stride=1, stride_axis=0)
            at = pl.ds(pl.multiple_of(g * 128, 128), 128)
            mats[at, 0:128] = jnp.where(lanes > rows, spin, 0.0).astype(BF)
            mats[at, 128:256] = jnp.where(lanes > rows, 0.0, spin).astype(BF)

    cross_over(2)

    @pl.when(zl == 2)
    def _():
        hand_on(heads, *tails)

    cross_over(3)

    @pl.when(zl == 3)
    def _():
        hand_on(tails[1])

    cross_over(4)
    for d in near:
        direct[d].wait_recv()
        relay[d].start()

    @pl.when(hi)
    def _():
        hand_on(heads)
        for k in (0, 1):
            ferry_out[k].wait_recv()
            ferry_on[k].start()

    for copy in second.values():
        copy.wait_recv()
    for copy in second_on.values():
        copy.start()

    for d in near:
        mate_direct[d].start()
    for copy in second_on.values():
        copy.wait_recv()
    for d in around:
        mate_second[d].start()
    for d in around:
        spread0[d].wait_recv()
    for d in near:
        wide0[d].start()
    for d in around:
        spread1[d].wait_recv()
    for d in near:
        wide1[d].start()
    mate_wide0[0].start()
    mate_wide1[0].start()
    for d in near:
        relay[d].wait_recv()
    mate_direct[2].start()

    def pass_wide():
        for d in near:
            wide0[d].wait_recv()
            relay0[d].start()
            wide1[d].wait_recv()
            relay1[d].start()
        for d in near:
            mate_wide0[d].start()
            mate_wide1[d].start()

    load_early.wait()
    for copy in load_rest[1:]:
        copy.wait()
    heads.wait_recv()
    got = jnp.where(s == 0, 0.0, pack[1].astype(F32))
    raw[0:16, :3072] = jnp.concatenate([got[0:8], got[0:8]], axis=0).astype(BF)
    raw[0:16, 3072:] = jnp.concatenate([got[8:16], got[8:16]], axis=0).astype(BF)

    @pl.loop(0, 16)
    def _(j):
        lane = j * 128
        product(lane, 0, 0)
        query[0:128, cols(lane, 128)] = conv(lane, 0, 2)
        query[128:256, cols(lane, 128)] = conv(lane, 128, 3)

    for copy in tails:
        copy.wait_recv()

    @pl.when(s == 0)
    def _():
        prod[0:128] = jnp.zeros((128, H), BF)

    group = lax.broadcasted_iota(jnp.int32, (128, 128), 1) // 16

    @pl.loop(0, 16)
    def _(j):
        lane = cols(j * 128, 128)
        pair = jnp.concatenate([prod[0:256, lane], prod[128:384, lane]], axis=1)
        spans = jnp.dot(mats[pl.ds(pl.multiple_of(j * 1024, 1024), 1024), :], pair, preferred_element_type=F32)
        for b in (0, 1):
            wave = spans[0:128, b * 128 : b * 128 + 128]
            for g in range(1, 8):
                wave = jnp.where(group == g, spans[g * 128 : g * 128 + 128, b * 128 : b * 128 + 128], wave)
            at = slice(b * 128, b * 128 + 128)
            wave = wave + skip[:, lane] * prod[b * 128 + 128 : b * 128 + 256, lane].astype(F32)
            gated[at, lane] = (query[at, lane] * wave).astype(BF)

    def tile(half, xx):
        return cols(xx * 512 + half * 256, 256)

    def project(hh, half, xx, blocks):
        left = jnp.concatenate([gated[:, cols((yy * 2 + hh) * 256, 256)] for yy in blocks], axis=1)
        right = jnp.concatenate([wbuf[yy, hh, :, half, xx, 0:128, :].reshape(256, 256) for yy in blocks], axis=0)
        return jnp.dot(left, right, preferred_element_type=F32)

    def gather_in(half, xx, blocks):
        at = tile(half, xx)
        stream[:, at] = stream[:, at] + project(o, half, xx, blocks)

    pass_wide()
    mate.wait_recv()
    for d in around:
        mate_direct[d].wait_recv()
    for d in around:
        mate_second[d].wait_recv()

    @pl.loop(0, 8)
    def _(n):
        half, xx = n // 4, lax.rem(n, 4)
        at = tile(half, xx)
        stream[:, at] = base[:, at].astype(F32) + project(h, half, xx, range(4))

    for group_of in (mate_wide0, mate_wide1):
        for copy in group_of.values():
            copy.wait_recv()

    @pl.loop(0, 3)
    def _(n):
        gather_in(1, lax.rem(x + 3 + n, 4), range(4))

    @pl.loop(0, 4)
    def _(n):
        gather_in(0, n, [lax.rem(y + 3 + k, 4) for k in range(3)])

    for d in near:
        relay0[d].wait_recv()
        mate_relay0[d].start()
        relay1[d].wait_recv()
        mate_relay1[d].start()
    for group_of in (mate_relay0, mate_relay1):
        for copy in group_of.values():
            copy.wait_recv()

    gather_in(1, lax.rem(x + 2, 4), range(4))

    def close(n, squares):
        gather_in(0, n, [lax.rem(y + 2, 4)])
        for half in (0, 1):
            total = stream[:, tile(half, n)]
            squares = squares + total[:, :128] * total[:, :128] + total[:, 128:] * total[:, 128:]
        return squares

    squares = lax.fori_loop(0, 4, close, jnp.zeros((256, 128), F32))
    scale = lax.rsqrt(jnp.sum(squares, axis=1, keepdims=True) / 2048.0 + 1e-05)

    @pl.loop(0, 8)
    def _(n):
        at = cols(n * 256, 256)
        gated[:, at] = (stream[:, at] * scale * gain[:, at]).astype(BF)

    words = jnp.concatenate(
        [wbuf[:, :, :, n % 2, n // 2, 128:160, :].reshape(512, 256) for n in range(8)], axis=1
    )
    logits = lax.dot_general(words, gated[...], (((1,), (1,)), ((), ())), preferred_element_type=F32)
    top = jnp.max(logits, axis=0, keepdims=True)
    total = top + jnp.log(jnp.sum(jnp.exp(logits - top), axis=0, keepdims=True))
    entry = lax.broadcasted_iota(jnp.int32, (512, 256), 0)
    out[...] = jnp.sum(jnp.where(entry == wanted[...], logits, 0.0), axis=0, keepdims=True) - total

    @pl.when(edge)
    def _():
        for copy in cross:
            copy.wait_send()

    @pl.when(passes)
    def _():
        for copy in onward:
            copy.wait_send()

    @pl.when(hi)
    def _():
        for copy in (*ferry_out, *ferry_on):
            copy.wait_send()

    @pl.when(jnp.logical_not(hi))
    def _():
        for copy in tails:
            copy.wait_send()

    for copy in (heads, mate):
        copy.wait_send()
    for group_of in (
        first, second, second_on, direct, relay, spread0, spread1, wide0, wide1, relay0, relay1, mate_direct, mate_second, mate_wide0, mate_wide1,
        mate_relay0, mate_relay1,
    ):
        for copy in group_of.values():
            copy.wait_send()


def body(qkv, resid, targets, short_filter, long_filter, skip, out_weight, gain, vocab_weight):
    vmem = pl.BlockSpec(memory_space=pltpu.VMEM)
    hbm = pl.BlockSpec(memory_space=pltpu.HBM)
    return pl.pallas_call(
        kernel,
        name="hyena_block",
        out_shape=jax.ShapeDtypeStruct((1, 256), F32),
        in_specs=[hbm] * 9,
        out_specs=vmem,
        scratch_shapes=[
            pltpu.VMEM((272, 6144), BF),
            pltpu.VMEM((4, 144, 128), F32),
            pltpu.VMEM((2, 16, 3072), BF),
            pltpu.VMEM((384, 2048), BF),
            pltpu.VMEM((2, 128, 1024), BF),
            pltpu.VMEM((256, 2048), F32),
            pltpu.VMEM((128, 128), F32),
            pltpu.VMEM((16384, 256), BF),
            pltpu.VMEM((256, 2048), BF),
            pltpu.VMEM((4, 2, 2, 2, 4, 160, 256), BF),
            pltpu.VMEM((256, 2048), F32),
            pltpu.VMEM((256, 2048), BF),
            pltpu.VMEM((7, 6144), F32),
            pltpu.VMEM((128, 128), BF),
            pltpu.VMEM((1, 2048), F32),
            pltpu.VMEM((1, 2048), F32),
            pltpu.VMEM((1, 256), jnp.int32),
            pltpu.SemaphoreType.DMA((32,)),
            pltpu.SemaphoreType.DMA((72,)),
            pltpu.SemaphoreType.DMA((72,)),
        ],
        compiler_params=pltpu.CompilerParams(
            collective_id=0, has_side_effects=True, vmem_limit_bytes=60 << 20
        ),
        cost_estimate=pl.CostEstimate(flops=7_000_000_000, bytes_accessed=20_000_000, transcendentals=131072),
    )(
        qkv, resid, targets, short_filter, long_filter, skip.reshape(1, -1), out_weight,
        gain.reshape(1, -1), vocab_weight,
    )


def solution(mesh):
    in_specs = (
        P("fsdp", "seq", None),
        P("fsdp", "seq", None),
        P("fsdp", "seq"),
        P(),
        P(),
        P(),
        P("fsdp", None),
        P(),
        P("fsdp", None),
    )
    out_specs = P("fsdp", "seq")
    return jax.shard_map(body, mesh=mesh, in_specs=in_specs, out_specs=out_specs, check_vma=False)
```

```python
import jax
import jax.numpy as jnp
from jax import lax
from jax.experimental import pallas as pl
from jax.experimental.pallas import tpu as pltpu
from jax.sharding import PartitionSpec as P

MESH = pl.DeviceIdType.MESH
BF = jnp.bfloat16
F32 = jnp.float32


def place(x, y, z, c):
    x, y, z = lax.rem(x + 4, 4), lax.rem(y + 4, 4), lax.rem(z + 16, 16)
    return (x * 8 + lax.rem(z, 8), (y * 2 + z // 8) * 2 + c)


def cols(start, size):
    return pl.ds(pl.multiple_of(start, 128), size)


def kernel(
    qkv, resid, targets, taps_in, longs_in, skip_in, ow, gain_in, vw, out,
    raw, ext, pack, prod, ferry, query, flips, mats, gated, wbuf, stream, base, taps, longs, skip, gain, wanted,
    local_sem, send_sem, recv_sem, gate_sem,
):
    H = 2048
    s, f = lax.axis_index("seq"), lax.axis_index("fsdp")
    x, zl = s // 8, lax.rem(s, 8)
    y, h, c = f // 4, lax.rem(f // 2, 2), lax.rem(f, 2)
    o = 1 - h
    z = h * 8 + zl
    lo, hi = zl == 0, zl == 7
    edge = jnp.logical_or(lo, hi)
    rank = jnp.where(zl < 5, zl, 7 - zl)
    outward = jnp.where(zl < 5, -1, 1)
    passes = jnp.logical_or(zl < 4, zl > 5)

    def xpeer(d):
        return place(x + d, y, z, c)

    def ypeer(d):
        return place(x, y + d, z, c)

    def back(a, d):
        return lax.rem(a + 4 - d, 4)

    outer, inner = place(x, y, z + outward, c), place(x, y, z - outward, c)
    sibling = (s, f + 1 - 2 * c)
    after, before = (lax.rem(s + 1, 32), f), (lax.rem(s + 31, 32), f)
    around, near = (1, 3, 2), (1, 3)

    barrier = pltpu.get_barrier_semaphore()

    def greet(device):
        pl.semaphore_signal(barrier, inc=1, device_id=device, device_id_type=MESH)

    for d in around:
        greet(xpeer(d))
        greet(ypeer(d))
    for device in (sibling, after, before, outer):
        greet(device)

    @pl.when(passes)
    def _():
        greet(inner)

    far = place(x, y, jnp.where(lo, z + 7, z - 7), c)

    @pl.when(edge)
    def _():
        greet(far)

    guard = zl == 5
    other = place(x, y, jnp.where(guard, z + 2, z - 2), c)

    @pl.when(jnp.logical_or(guard, hi))
    def _():
        greet(other)

    loads = []

    def load(src, dst):
        copy = pltpu.make_async_copy(src, dst, local_sem.at[len(loads)])
        copy.start()
        loads.append(copy)
        return copy

    def own(half, strip):
        at = pl.ds(strip * 512 + half * 256, 256)
        return [
            load(ow.at[:, at], wbuf.at[y, h, c, half, strip, 0:128]),
            load(vw.at[:, at], wbuf.at[y, h, c, half, strip, 128:160]),
        ]

    load_own = [copy for half in (1, 0) for strip in range(4) for copy in own(half, strip)]
    load_late = load(qkv.at[0, 112:256, H:], raw.at[128:272, H:])
    load_taps = load(taps_in, taps)
    load_early = load(qkv.at[0, 0:112, H:], raw.at[16:128, H:])
    load_q = load(qkv.at[0, :, :H], raw.at[16:272, :H])
    load_rest = [
        load(longs_in, longs), load(skip_in, skip), load(gain_in, gain), load(targets, wanted), load(resid.at[0], base),
    ]

    count = [0]

    def send(src, device, dst=None, slot=None):
        n = count[0]
        count[0] += 1
        return pltpu.make_async_remote_copy(
            src_ref=src, dst_ref=src if dst is None else dst, send_sem=send_sem.at[n],
            recv_sem=recv_sem.at[n if slot is None else slot], device_id=device, device_id_type=MESH,
        )

    def strip(yy, hh, half, xx):
        return wbuf.at[yy, hh, c, half, xx]

    def whole(yy, hh, half):
        return wbuf.at[yy, hh, c, half]

    def column(hh, half, xx):
        return wbuf.at[:, hh, c, half, xx]

    def half_whole(yy, hh, d):
        return wbuf.at[yy, hh, c, 0, 0:2] if d == 1 else wbuf.at[yy, hh, c, 0, 2:4]

    def half_column(xx, d):
        return wbuf.at[0:2, o, c, 1, xx] if d == 1 else wbuf.at[2:4, o, c, 1, xx]

    def piece(hh, k):
        return wbuf.at[y, hh, c, k // 2, x, pl.ds(k % 2 * 80, 80)]

    cross, onward = [], []
    for k in range(4):
        slot = count[0]
        cross.append(send(piece(h, k), outer, slot=slot))
        onward.append(send(piece(o, k), inner, slot=slot))
    heads = send(pack.at[0], after, dst=pack.at[1])
    tails, ferry_out, ferry_on = [], [], []
    for k in (0, 1):
        at, slot = pl.ds(k * 1024, 1024), count[0]
        tails.append(send(prod.at[256:384, at], after, dst=prod.at[0:128, at]))
        ferry_out.append(send(prod.at[256:384, at], xpeer(1), dst=ferry.at[k]))
        ferry_on.append(send(ferry.at[k], far, dst=prod.at[0:128, at], slot=slot))
    first = {d: send(strip(y, h, 1, x), ypeer(d)) for d in around}
    second = {(k, d): send(strip(back(y, k), h, 1, x), xpeer(d)) for k in around for d in near}
    second_on = {
        (k, d): send(strip(back(y, k), h, 1, back(x, d)), xpeer(d)) for k, d in ((1, 1), (3, 3))
    }
    for d in near:
        second_on[2, d] = send(wbuf.at[back(y, 2), h, c, 1, back(x, d), pl.ds(d // 2 * 80, 80)], xpeer(d))
    direct = {d: send(whole(y, h, 0), ypeer(d)) for d in near}
    relay = {d: send(half_whole(back(y, d), h, d), ypeer(d)) for d in near}
    spread0 = {d: send(strip(y, o, 0, x), xpeer(d)) for d in around}
    spread1 = {d: send(strip(y, o, 1, x), ypeer(d)) for d in around}
    wide0 = {d: send(whole(y, o, 0), ypeer(d)) for d in near}
    wide1 = {d: send(column(o, 1, x), xpeer(d)) for d in near}
    relay0 = {d: send(half_whole(back(y, d), o, d), ypeer(d)) for d in near}
    relay1 = {d: send(half_column(back(x, d), d), xpeer(d)) for d in near}
    mate = send(wbuf.at[y, h, c], sibling)
    mate_direct = {d: send(whole(back(y, d), h, 0), sibling) for d in around}
    mate_second = {d: send(whole(back(y, d), h, 1), sibling) for d in around}
    mate_wide0 = {d: send(whole(back(y, d), o, 0), sibling) for d in (0,) + near}
    mate_wide1 = {d: send(column(o, 1, back(x, d)), sibling) for d in (0,) + near}
    mate_relay0 = {d: send(half_whole(back(y, 2), o, d), sibling) for d in near}
    mate_relay1 = {d: send(half_column(back(x, 2), d), sibling) for d in near}

    def conv(col, top, spot):
        ext[spot] = raw[top : top + 144, cols(col, 128)].astype(F32)
        total = jnp.zeros((128, 128), F32)
        for lag in range(7):
            total = total + taps[lag : lag + 1, cols(col, 128)] * ext[spot, 16 - lag : 144 - lag]
        return total

    def product(lane, top, spot):
        k = conv(H + lane, top, spot)
        v = conv(2 * H + lane, top, spot + 1)
        prod[128 + top : 256 + top, cols(lane, 128)] = (k * v).astype(BF)

    def late_rows():
        load_late.wait()
        load_taps.wait()
        load_q.wait()
        last = raw[256:272].astype(F32)[8:16]
        pack[0] = jnp.concatenate([last[:, :3072], last[:, 3072:]], axis=0).astype(BF)

        @pl.loop(0, 16)
        def _(j):
            product(j * 128, 128, 0)

    pl.when(hi)(late_rows)
    for copy in load_own:
        copy.wait()
    pl.semaphore_wait(barrier, 10 + jnp.where(passes, 1, 0) + jnp.where(edge, 1, 0) + jnp.where(jnp.logical_or(guard, hi), 1, 0))

    @pl.when(edge)
    def _():
        for copy in cross:
            copy.start()

    for d in around:
        first[d].start()
    pl.when(jnp.logical_not(hi))(late_rows)

    def hand_on(*copies):
        for copy in copies:
            copy.start()

    @pl.when(hi)
    def _():
        hand_on(*ferry_out)

    @pl.when(jnp.logical_or(zl == 3, jnp.logical_not(passes)))
    def _():
        hand_on(heads, tails[0])

    @pl.when(jnp.logical_not(passes))
    def _():
        hand_on(tails[1])

    for d in near:
        direct[d].start()
    mate.start()

    def cross_over(level):
        @pl.when(rank == level)
        def _():
            for k in range(4):
                onward[k].wait_recv()
                if level < 4:
                    pl.when(passes)(onward[k].start)
                if k % 2:
                    for d in around:
                        (spread0, spread1)[k // 2][d].start()

    cross_over(0)

    @pl.when(lo)
    def _():
        hand_on(heads, *tails)

    for k in around:
        first[k].wait_recv()
        pl.when(jnp.logical_not(hi))(second[k, 1].start)
        second[k, 3].start()

    cross_over(1)

    @pl.when(rank == 1)
    def _():
        hand_on(heads, *tails)

    rows = lax.broadcasted_iota(jnp.int32, (128, 128), 0)
    lanes = lax.broadcasted_iota(jnp.int32, (128, 128), 1)
    turn = jnp.where(lax.rem(rows + lanes, 128) == 0, 1.0, 0.0).astype(BF)
    load_rest[0].wait()
    flips[...] = jnp.dot(longs[...], turn, preferred_element_type=F32)

    @pl.loop(0, 16)
    def _(j):
        for k in range(8):
            g = j * 8 + k
            spin = pltpu.roll(jnp.broadcast_to(flips[pl.ds(g, 1), :], (128, 128)), 0, 1, stride=1, stride_axis=0)
            at = pl.ds(pl.multiple_of(g * 128, 128), 128)
            mats[at, 0:128] = jnp.where(lanes > rows, spin, 0.0).astype(BF)
            mats[at, 128:256] = jnp.where(lanes > rows, 0.0, spin).astype(BF)

    cross_over(2)

    @pl.when(guard)
    def _():
        pl.semaphore_signal(gate_sem, inc=1, device_id=other, device_id_type=MESH)

    @pl.when(zl == 2)
    def _():
        hand_on(heads, *tails)

    cross_over(3)

    @pl.when(zl == 3)
    def _():
        hand_on(tails[1])

    cross_over(4)
    for d in near:
        direct[d].wait_recv()
        relay[d].start()

    @pl.when(hi)
    def _():
        pl.semaphore_wait(gate_sem, 1)
        hand_on(heads)
        for k in (0, 1):
            ferry_out[k].wait_recv()
            ferry_on[k].start()
        for k in around:
            second[k, 1].start()

    for copy in second.values():
        copy.wait_recv()
    for copy in second_on.values():
        copy.start()

    for d in near:
        mate_direct[d].start()
    for copy in second_on.values():
        copy.wait_recv()
    for d in around:
        mate_second[d].start()
    for d in around:
        spread0[d].wait_recv()
    for d in near:
        wide0[d].start()
    for d in around:
        spread1[d].wait_recv()
    for d in near:
        wide1[d].start()
    mate_wide0[0].start()
    mate_wide1[0].start()
    for d in near:
        relay[d].wait_recv()
    mate_direct[2].start()

    def pass_wide():
        for d in near:
            wide0[d].wait_recv()
            relay0[d].start()
            wide1[d].wait_recv()
            relay1[d].start()
        for d in near:
            mate_wide0[d].start()
            mate_wide1[d].start()

    load_early.wait()
    for copy in load_rest[1:]:
        copy.wait()
    heads.wait_recv()
    got = jnp.where(s == 0, 0.0, pack[1].astype(F32))
    raw[0:16, :3072] = jnp.concatenate([got[0:8], got[0:8]], axis=0).astype(BF)
    raw[0:16, 3072:] = jnp.concatenate([got[8:16], got[8:16]], axis=0).astype(BF)

    @pl.loop(0, 16)
    def _(j):
        lane = j * 128
        product(lane, 0, 0)
        query[0:128, cols(lane, 128)] = conv(lane, 0, 2)
        query[128:256, cols(lane, 128)] = conv(lane, 128, 3)

    pl.when(lo)(pass_wide)
    for copy in tails:
        copy.wait_recv()

    @pl.when(s == 0)
    def _():
        prod[0:128] = jnp.zeros((128, H), BF)

    group = lax.broadcasted_iota(jnp.int32, (128, 128), 1) // 16

    @pl.loop(0, 16)
    def _(j):
        lane = cols(j * 128, 128)
        pair = jnp.concatenate([prod[0:256, lane], prod[128:384, lane]], axis=1)
        spans = jnp.dot(mats[pl.ds(pl.multiple_of(j * 1024, 1024), 1024), :], pair, preferred_element_type=F32)
        for b in (0, 1):
            wave = spans[0:128, b * 128 : b * 128 + 128]
            for g in range(1, 8):
                wave = jnp.where(group == g, spans[g * 128 : g * 128 + 128, b * 128 : b * 128 + 128], wave)
            at = slice(b * 128, b * 128 + 128)
            wave = wave + skip[:, lane] * prod[b * 128 + 128 : b * 128 + 256, lane].astype(F32)
            gated[at, lane] = (query[at, lane] * wave).astype(BF)

    def tile(half, xx):
        return cols(xx * 512 + half * 256, 256)

    def project(hh, half, xx, blocks):
        left = jnp.concatenate([gated[:, cols((yy * 2 + hh) * 256, 256)] for yy in blocks], axis=1)
        right = jnp.concatenate([wbuf[yy, hh, :, half, xx, 0:128, :].reshape(256, 256) for yy in blocks], axis=0)
        return jnp.dot(left, right, preferred_element_type=F32)

    def gather_in(half, xx, blocks):
        at = tile(half, xx)
        stream[:, at] = stream[:, at] + project(o, half, xx, blocks)

    pl.when(jnp.logical_not(lo))(pass_wide)
    mate.wait_recv()
    for d in around:
        mate_direct[d].wait_recv()
    for d in around:
        mate_second[d].wait_recv()

    @pl.loop(0, 8)
    def _(n):
        half, xx = n // 4, lax.rem(n, 4)
        at = tile(half, xx)
        stream[:, at] = base[:, at].astype(F32) + project(h, half, xx, range(4))

    for group_of in (mate_wide0, mate_wide1):
        for copy in group_of.values():
            copy.wait_recv()

    @pl.loop(0, 3)
    def _(n):
        gather_in(1, lax.rem(x + 3 + n, 4), range(4))

    @pl.loop(0, 4)
    def _(n):
        gather_in(0, n, [lax.rem(y + 3 + k, 4) for k in range(3)])

    for d in near:
        relay0[d].wait_recv()
        mate_relay0[d].start()
        relay1[d].wait_recv()
        mate_relay1[d].start()
    for group_of in (mate_relay0, mate_relay1):
        for copy in group_of.values():
            copy.wait_recv()

    gather_in(1, lax.rem(x + 2, 4), range(4))

    def close(n, squares):
        gather_in(0, n, [lax.rem(y + 2, 4)])
        for half in (0, 1):
            total = stream[:, tile(half, n)]
            squares = squares + total[:, :128] * total[:, :128] + total[:, 128:] * total[:, 128:]
        return squares

    squares = lax.fori_loop(0, 4, close, jnp.zeros((256, 128), F32))
    scale = lax.rsqrt(jnp.sum(squares, axis=1, keepdims=True) / 2048.0 + 1e-05)

    @pl.loop(0, 8)
    def _(n):
        at = cols(n * 256, 256)
        gated[:, at] = (stream[:, at] * scale * gain[:, at]).astype(BF)

    words = jnp.concatenate(
        [wbuf[:, :, :, n % 2, n // 2, 128:160, :].reshape(512, 256) for n in range(8)], axis=1
    )
    logits = lax.dot_general(words, gated[...], (((1,), (1,)), ((), ())), preferred_element_type=F32)
    top = jnp.max(logits, axis=0, keepdims=True)
    total = top + jnp.log(jnp.sum(jnp.exp(logits - top), axis=0, keepdims=True))
    entry = lax.broadcasted_iota(jnp.int32, (512, 256), 0)
    out[...] = jnp.sum(jnp.where(entry == wanted[...], logits, 0.0), axis=0, keepdims=True) - total

    @pl.when(edge)
    def _():
        for copy in cross:
            copy.wait_send()

    @pl.when(passes)
    def _():
        for copy in onward:
            copy.wait_send()

    @pl.when(hi)
    def _():
        for copy in (*ferry_out, *ferry_on):
            copy.wait_send()

    @pl.when(jnp.logical_not(hi))
    def _():
        for copy in tails:
            copy.wait_send()

    for copy in (heads, mate):
        copy.wait_send()
    for group_of in (
        first, second, second_on, direct, relay, spread0, spread1, wide0, wide1, relay0, relay1, mate_direct, mate_second, mate_wide0, mate_wide1,
        mate_relay0, mate_relay1,
    ):
        for copy in group_of.values():
            copy.wait_send()


def body(qkv, resid, targets, short_filter, long_filter, skip, out_weight, gain, vocab_weight):
    vmem = pl.BlockSpec(memory_space=pltpu.VMEM)
    hbm = pl.BlockSpec(memory_space=pltpu.HBM)
    return pl.pallas_call(
        kernel,
        name="hyena_block",
        out_shape=jax.ShapeDtypeStruct((1, 256), F32),
        in_specs=[hbm] * 9,
        out_specs=vmem,
        scratch_shapes=[
            pltpu.VMEM((272, 6144), BF),
            pltpu.VMEM((4, 144, 128), F32),
            pltpu.VMEM((2, 16, 3072), BF),
            pltpu.VMEM((384, 2048), BF),
            pltpu.VMEM((2, 128, 1024), BF),
            pltpu.VMEM((256, 2048), F32),
            pltpu.VMEM((128, 128), F32),
            pltpu.VMEM((16384, 256), BF),
            pltpu.VMEM((256, 2048), BF),
            pltpu.VMEM((4, 2, 2, 2, 4, 160, 256), BF),
            pltpu.VMEM((256, 2048), F32),
            pltpu.VMEM((256, 2048), BF),
            pltpu.VMEM((7, 6144), F32),
            pltpu.VMEM((128, 128), BF),
            pltpu.VMEM((1, 2048), F32),
            pltpu.VMEM((1, 2048), F32),
            pltpu.VMEM((1, 256), jnp.int32),
            pltpu.SemaphoreType.DMA((32,)),
            pltpu.SemaphoreType.DMA((72,)),
            pltpu.SemaphoreType.DMA((72,)),
            pltpu.SemaphoreType.REGULAR,
        ],
        compiler_params=pltpu.CompilerParams(
            collective_id=0, has_side_effects=True, vmem_limit_bytes=60 << 20
        ),
        cost_estimate=pl.CostEstimate(flops=7_000_000_000, bytes_accessed=20_000_000, transcendentals=131072),
    )(
        qkv, resid, targets, short_filter, long_filter, skip.reshape(1, -1), out_weight,
        gain.reshape(1, -1), vocab_weight,
    )


def solution(mesh):
    in_specs = (
        P("fsdp", "seq", None),
        P("fsdp", "seq", None),
        P("fsdp", "seq"),
        P(),
        P(),
        P(),
        P("fsdp", None),
        P(),
        P("fsdp", None),
    )
    out_specs = P("fsdp", "seq")
    return jax.shard_map(body, mesh=mesh, in_specs=in_specs, out_specs=out_specs, check_vma=False)
```

```python
import jax
import jax.numpy as jnp
from jax import lax
from jax.experimental import pallas as pl
from jax.experimental.pallas import tpu as pltpu
from jax.sharding import PartitionSpec as P

MESH = pl.DeviceIdType.MESH
BF = jnp.bfloat16
F32 = jnp.float32


def place(x, y, z, c):
    x, y, z = lax.rem(x + 4, 4), lax.rem(y + 4, 4), lax.rem(z + 16, 16)
    return (x * 8 + lax.rem(z, 8), (y * 2 + z // 8) * 2 + c)


def cols(start, size):
    return pl.ds(pl.multiple_of(start, 128), size)


def kernel(
    qkv, resid, targets, taps_in, longs_in, skip_in, ow, gain_in, vw, out,
    raw, ext, pack, prod, ferry, query, flips, mats, gated, wbuf, stream, base, taps, longs, skip, gain, wanted,
    local_sem, send_sem, recv_sem, gate_sem,
):
    H = 2048
    s, f = lax.axis_index("seq"), lax.axis_index("fsdp")
    x, zl = s // 8, lax.rem(s, 8)
    y, h, c = f // 4, lax.rem(f // 2, 2), lax.rem(f, 2)
    o = 1 - h
    z = h * 8 + zl
    lo, hi = zl == 0, zl == 7
    edge = jnp.logical_or(lo, hi)
    rank = jnp.where(zl < 5, zl, 7 - zl)
    outward = jnp.where(zl < 5, -1, 1)
    passes = jnp.logical_or(zl < 4, zl > 5)

    def xpeer(d):
        return place(x + d, y, z, c)

    def ypeer(d):
        return place(x, y + d, z, c)

    def back(a, d):
        return lax.rem(a + 4 - d, 4)

    outer, inner = place(x, y, z + outward, c), place(x, y, z - outward, c)
    sibling = (s, f + 1 - 2 * c)
    after, before = (lax.rem(s + 1, 32), f), (lax.rem(s + 31, 32), f)
    around, near = (1, 3, 2), (1, 3)

    barrier = pltpu.get_barrier_semaphore()

    def greet(device):
        pl.semaphore_signal(barrier, inc=1, device_id=device, device_id_type=MESH)

    for d in around:
        greet(xpeer(d))
        greet(ypeer(d))
    for device in (sibling, after, before, outer):
        greet(device)

    @pl.when(passes)
    def _():
        greet(inner)

    far = place(x, y, jnp.where(lo, z + 7, z - 7), c)

    @pl.when(edge)
    def _():
        greet(far)

    guard = zl == 6

    loads = []

    def load(src, dst):
        copy = pltpu.make_async_copy(src, dst, local_sem.at[len(loads)])
        copy.start()
        loads.append(copy)
        return copy

    def own(half, strip):
        at = pl.ds(strip * 512 + half * 256, 256)
        return [
            load(ow.at[:, at], wbuf.at[y, h, c, half, strip, 0:128]),
            load(vw.at[:, at], wbuf.at[y, h, c, half, strip, 128:160]),
        ]

    load_own = [copy for half in (1, 0) for strip in range(4) for copy in own(half, strip)]
    load_late = load(qkv.at[0, 112:256, H:], raw.at[128:272, H:])
    load_taps = load(taps_in, taps)
    load_early = load(qkv.at[0, 0:112, H:], raw.at[16:128, H:])
    load_q = load(qkv.at[0, :, :H], raw.at[16:272, :H])
    load_rest = [
        load(longs_in, longs), load(skip_in, skip), load(gain_in, gain), load(targets, wanted), load(resid.at[0], base),
    ]

    count = [0]

    def send(src, device, dst=None, slot=None):
        n = count[0]
        count[0] += 1
        return pltpu.make_async_remote_copy(
            src_ref=src, dst_ref=src if dst is None else dst, send_sem=send_sem.at[n],
            recv_sem=recv_sem.at[n if slot is None else slot], device_id=device, device_id_type=MESH,
        )

    def strip(yy, hh, half, xx):
        return wbuf.at[yy, hh, c, half, xx]

    def whole(yy, hh, half):
        return wbuf.at[yy, hh, c, half]

    def column(hh, half, xx):
        return wbuf.at[:, hh, c, half, xx]

    def half_whole(yy, hh, d):
        return wbuf.at[yy, hh, c, 0, 0:2] if d == 1 else wbuf.at[yy, hh, c, 0, 2:4]

    def half_column(xx, d):
        return wbuf.at[0:2, o, c, 1, xx] if d == 1 else wbuf.at[2:4, o, c, 1, xx]

    def piece(hh, k):
        return wbuf.at[y, hh, c, k // 2, x, pl.ds(k % 2 * 80, 80)]

    cross, onward = [], []
    for k in range(4):
        slot = count[0]
        cross.append(send(piece(h, k), outer, slot=slot))
        onward.append(send(piece(o, k), inner, slot=slot))
    heads = send(pack.at[0], after, dst=pack.at[1])
    tails, ferry_out, ferry_on = [], [], []
    for k in (0, 1):
        at, slot = pl.ds(k * 1024, 1024), count[0]
        tails.append(send(prod.at[256:384, at], after, dst=prod.at[0:128, at]))
        ferry_out.append(send(prod.at[256:384, at], xpeer(1), dst=ferry.at[k]))
        ferry_on.append(send(ferry.at[k], far, dst=prod.at[0:128, at], slot=slot))
    first = {d: send(strip(y, h, 1, x), ypeer(d)) for d in around}
    second = {(k, d): send(strip(back(y, k), h, 1, x), xpeer(d)) for k in around for d in near}
    second_on = {
        (k, d): send(strip(back(y, k), h, 1, back(x, d)), xpeer(d)) for k, d in ((1, 1), (3, 3))
    }
    for d in near:
        second_on[2, d] = send(wbuf.at[back(y, 2), h, c, 1, back(x, d), pl.ds(d // 2 * 80, 80)], xpeer(d))
    direct = {d: send(whole(y, h, 0), ypeer(d)) for d in near}
    relay = {d: send(half_whole(back(y, d), h, d), ypeer(d)) for d in near}
    spread0 = {d: send(strip(y, o, 0, x), xpeer(d)) for d in around}
    spread1 = {d: send(strip(y, o, 1, x), ypeer(d)) for d in around}
    wide0 = {d: send(whole(y, o, 0), ypeer(d)) for d in near}
    wide1 = {d: send(column(o, 1, x), xpeer(d)) for d in near}
    relay0 = {d: send(half_whole(back(y, d), o, d), ypeer(d)) for d in near}
    relay1 = {d: send(half_column(back(x, d), d), xpeer(d)) for d in near}
    mate = send(wbuf.at[y, h, c], sibling)
    mate_direct = {d: send(whole(back(y, d), h, 0), sibling) for d in around}
    mate_second = {d: send(whole(back(y, d), h, 1), sibling) for d in around}
    mate_wide0 = {d: send(whole(back(y, d), o, 0), sibling) for d in (0,) + near}
    mate_wide1 = {d: send(column(o, 1, back(x, d)), sibling) for d in (0,) + near}
    mate_relay0 = {d: send(half_whole(back(y, 2), o, d), sibling) for d in near}
    mate_relay1 = {d: send(half_column(back(x, 2), d), sibling) for d in near}

    def conv(col, top, spot):
        ext[spot] = raw[top : top + 144, cols(col, 128)].astype(F32)
        total = jnp.zeros((128, 128), F32)
        for lag in range(7):
            total = total + taps[lag : lag + 1, cols(col, 128)] * ext[spot, 16 - lag : 144 - lag]
        return total

    def product(lane, top, spot):
        k = conv(H + lane, top, spot)
        v = conv(2 * H + lane, top, spot + 1)
        prod[128 + top : 256 + top, cols(lane, 128)] = (k * v).astype(BF)

    def late_rows():
        load_late.wait()
        load_taps.wait()
        load_q.wait()
        last = raw[256:272].astype(F32)[8:16]
        pack[0] = jnp.concatenate([last[:, :3072], last[:, 3072:]], axis=0).astype(BF)

        @pl.loop(0, 16)
        def _(j):
            product(j * 128, 128, 0)

    pl.when(hi)(late_rows)
    for copy in load_own:
        copy.wait()
    pl.semaphore_wait(barrier, 10 + jnp.where(passes, 1, 0) + jnp.where(edge, 1, 0))

    @pl.when(edge)
    def _():
        for copy in cross:
            copy.start()

    for d in around:
        first[d].start()
    pl.when(jnp.logical_not(hi))(late_rows)

    def hand_on(*copies):
        for copy in copies:
            copy.start()

    @pl.when(hi)
    def _():
        hand_on(*ferry_out)

    @pl.when(jnp.logical_or(zl == 3, jnp.logical_not(passes)))
    def _():
        hand_on(heads, tails[0])

    @pl.when(jnp.logical_not(passes))
    def _():
        hand_on(tails[1])

    for d in near:
        direct[d].start()
    mate.start()

    def cross_over(level):
        @pl.when(rank == level)
        def _():
            for k in range(4):
                onward[k].wait_recv()
                if level < 4:
                    pl.when(passes)(onward[k].start)
                if k % 2:
                    for d in around:
                        (spread0, spread1)[k // 2][d].start()

    cross_over(0)

    @pl.when(lo)
    def _():
        hand_on(heads, *tails)

    for k in around:
        first[k].wait_recv()
        pl.when(jnp.logical_not(hi))(second[k, 1].start)
        second[k, 3].start()

    cross_over(1)

    @pl.when(rank == 1)
    def _():
        hand_on(heads, *tails)

    rows = lax.broadcasted_iota(jnp.int32, (128, 128), 0)
    lanes = lax.broadcasted_iota(jnp.int32, (128, 128), 1)
    turn = jnp.where(lax.rem(rows + lanes, 128) == 0, 1.0, 0.0).astype(BF)
    load_rest[0].wait()
    flips[...] = jnp.dot(longs[...], turn, preferred_element_type=F32)

    @pl.loop(0, 16)
    def _(j):
        for k in range(8):
            g = j * 8 + k
            spin = pltpu.roll(jnp.broadcast_to(flips[pl.ds(g, 1), :], (128, 128)), 0, 1, stride=1, stride_axis=0)
            at = pl.ds(pl.multiple_of(g * 128, 128), 128)
            mats[at, 0:128] = jnp.where(lanes > rows, spin, 0.0).astype(BF)
            mats[at, 128:256] = jnp.where(lanes > rows, 0.0, spin).astype(BF)

    cross_over(2)

    @pl.when(guard)
    def _():
        for copy in onward:
            copy.wait_send()
        pl.semaphore_signal(gate_sem, inc=1, device_id=outer, device_id_type=MESH)

    @pl.when(zl == 2)
    def _():
        hand_on(heads, *tails)

    cross_over(3)

    @pl.when(zl == 3)
    def _():
        hand_on(tails[1])

    cross_over(4)
    for d in near:
        direct[d].wait_recv()
        relay[d].start()

    @pl.when(hi)
    def _():
        pl.semaphore_wait(gate_sem, 1)
        hand_on(heads)
        for k in (0, 1):
            ferry_out[k].wait_recv()
            ferry_on[k].start()
        for k in around:
            second[k, 1].start()

    for copy in second.values():
        copy.wait_recv()
    for copy in second_on.values():
        copy.start()

    for d in near:
        mate_direct[d].start()
    for copy in second_on.values():
        copy.wait_recv()
    for d in around:
        mate_second[d].start()
    for d in around:
        spread0[d].wait_recv()
    for d in near:
        wide0[d].start()
    for d in around:
        spread1[d].wait_recv()
    for d in near:
        wide1[d].start()
    mate_wide0[0].start()
    mate_wide1[0].start()
    for d in near:
        relay[d].wait_recv()
    mate_direct[2].start()

    def pass_wide():
        for d in near:
            wide0[d].wait_recv()
            relay0[d].start()
            wide1[d].wait_recv()
            relay1[d].start()
        for d in near:
            mate_wide0[d].start()
            mate_wide1[d].start()

    load_early.wait()
    for copy in load_rest[1:]:
        copy.wait()
    heads.wait_recv()
    got = jnp.where(s == 0, 0.0, pack[1].astype(F32))
    raw[0:16, :3072] = jnp.concatenate([got[0:8], got[0:8]], axis=0).astype(BF)
    raw[0:16, 3072:] = jnp.concatenate([got[8:16], got[8:16]], axis=0).astype(BF)

    @pl.loop(0, 16)
    def _(j):
        lane = j * 128
        product(lane, 0, 0)
        query[0:128, cols(lane, 128)] = conv(lane, 0, 2)
        query[128:256, cols(lane, 128)] = conv(lane, 128, 3)

    def pass_relays():
        for d in near:
            relay0[d].wait_recv()
            mate_relay0[d].start()
            relay1[d].wait_recv()
            mate_relay1[d].start()

    @pl.when(lo)
    def _():
        pass_wide()
        pass_relays()

    for copy in tails:
        copy.wait_recv()

    @pl.when(s == 0)
    def _():
        prod[0:128] = jnp.zeros((128, H), BF)

    group = lax.broadcasted_iota(jnp.int32, (128, 128), 1) // 16

    @pl.loop(0, 16, unroll=2)
    def _(j):
        lane = cols(j * 128, 128)
        pair = jnp.concatenate([prod[0:256, lane], prod[128:384, lane]], axis=1)
        spans = jnp.dot(mats[pl.ds(pl.multiple_of(j * 1024, 1024), 1024), :], pair, preferred_element_type=F32)
        for b in (0, 1):
            wave = spans[0:128, b * 128 : b * 128 + 128]
            for g in range(1, 8):
                wave = jnp.where(group == g, spans[g * 128 : g * 128 + 128, b * 128 : b * 128 + 128], wave)
            at = slice(b * 128, b * 128 + 128)
            wave = wave + skip[:, lane] * prod[b * 128 + 128 : b * 128 + 256, lane].astype(F32)
            gated[at, lane] = (query[at, lane] * wave).astype(BF)

    def tile(half, xx):
        return cols(xx * 512 + half * 256, 256)

    def project(hh, half, xx, blocks):
        left = jnp.concatenate([gated[:, cols((yy * 2 + hh) * 256, 256)] for yy in blocks], axis=1)
        right = jnp.concatenate([wbuf[yy, hh, :, half, xx, 0:128, :].reshape(256, 256) for yy in blocks], axis=0)
        return jnp.dot(left, right, preferred_element_type=F32)

    def gather_in(half, xx, blocks):
        at = tile(half, xx)
        stream[:, at] = stream[:, at] + project(o, half, xx, blocks)

    pl.when(jnp.logical_not(lo))(pass_wide)
    mate.wait_recv()
    for d in around:
        mate_direct[d].wait_recv()
    for d in around:
        mate_second[d].wait_recv()

    @pl.loop(0, 8, unroll=2)
    def _(n):
        half, xx = n // 4, lax.rem(n, 4)
        at = tile(half, xx)
        stream[:, at] = base[:, at].astype(F32) + project(h, half, xx, range(4))

    for group_of in (mate_wide0, mate_wide1):
        for copy in group_of.values():
            copy.wait_recv()

    @pl.loop(0, 3, unroll=3)
    def _(n):
        gather_in(1, lax.rem(x + 3 + n, 4), range(4))

    @pl.loop(0, 4, unroll=4)
    def _(n):
        gather_in(0, n, [lax.rem(y + 3 + k, 4) for k in range(3)])

    pl.when(jnp.logical_not(lo))(pass_relays)
    for group_of in (mate_relay0, mate_relay1):
        for copy in group_of.values():
            copy.wait_recv()

    gather_in(1, lax.rem(x + 2, 4), range(4))

    def close(n, squares):
        gather_in(0, n, [lax.rem(y + 2, 4)])
        for half in (0, 1):
            total = stream[:, tile(half, n)]
            squares = squares + total[:, :128] * total[:, :128] + total[:, 128:] * total[:, 128:]
        return squares

    squares = lax.fori_loop(0, 4, close, jnp.zeros((256, 128), F32), unroll=2)
    scale = lax.rsqrt(jnp.sum(squares, axis=1, keepdims=True) / 2048.0 + 1e-05)

    @pl.loop(0, 8, unroll=2)
    def _(n):
        at = cols(n * 256, 256)
        gated[:, at] = (stream[:, at] * scale * gain[:, at]).astype(BF)

    words = jnp.concatenate(
        [wbuf[:, :, :, n % 2, n // 2, 128:160, :].reshape(512, 256) for n in range(8)], axis=1
    )
    logits = lax.dot_general(words, gated[...], (((1,), (1,)), ((), ())), preferred_element_type=F32)
    top = jnp.max(logits, axis=0, keepdims=True)
    total = top + jnp.log(jnp.sum(jnp.exp(logits - top), axis=0, keepdims=True))
    entry = lax.broadcasted_iota(jnp.int32, (512, 256), 0)
    out[...] = jnp.sum(jnp.where(entry == wanted[...], logits, 0.0), axis=0, keepdims=True) - total

    @pl.when(edge)
    def _():
        for copy in cross:
            copy.wait_send()

    @pl.when(jnp.logical_and(passes, jnp.logical_not(guard)))
    def _():
        for copy in onward:
            copy.wait_send()

    @pl.when(hi)
    def _():
        for copy in (*ferry_out, *ferry_on):
            copy.wait_send()

    @pl.when(jnp.logical_not(hi))
    def _():
        for copy in tails:
            copy.wait_send()

    for copy in (heads, mate):
        copy.wait_send()
    for group_of in (
        first, second, second_on, direct, relay, spread0, spread1, wide0, wide1, relay0, relay1, mate_direct, mate_second, mate_wide0, mate_wide1,
        mate_relay0, mate_relay1,
    ):
        for copy in group_of.values():
            copy.wait_send()


def body(qkv, resid, targets, short_filter, long_filter, skip, out_weight, gain, vocab_weight):
    vmem = pl.BlockSpec(memory_space=pltpu.VMEM)
    hbm = pl.BlockSpec(memory_space=pltpu.HBM)
    return pl.pallas_call(
        kernel,
        name="hyena_block",
        out_shape=jax.ShapeDtypeStruct((1, 256), F32),
        in_specs=[hbm] * 9,
        out_specs=vmem,
        scratch_shapes=[
            pltpu.VMEM((272, 6144), BF),
            pltpu.VMEM((4, 144, 128), F32),
            pltpu.VMEM((2, 16, 3072), BF),
            pltpu.VMEM((384, 2048), BF),
            pltpu.VMEM((2, 128, 1024), BF),
            pltpu.VMEM((256, 2048), F32),
            pltpu.VMEM((128, 128), F32),
            pltpu.VMEM((16384, 256), BF),
            pltpu.VMEM((256, 2048), BF),
            pltpu.VMEM((4, 2, 2, 2, 4, 160, 256), BF),
            pltpu.VMEM((256, 2048), F32),
            pltpu.VMEM((256, 2048), BF),
            pltpu.VMEM((7, 6144), F32),
            pltpu.VMEM((128, 128), BF),
            pltpu.VMEM((1, 2048), F32),
            pltpu.VMEM((1, 2048), F32),
            pltpu.VMEM((1, 256), jnp.int32),
            pltpu.SemaphoreType.DMA((32,)),
            pltpu.SemaphoreType.DMA((72,)),
            pltpu.SemaphoreType.DMA((72,)),
            pltpu.SemaphoreType.REGULAR,
        ],
        compiler_params=pltpu.CompilerParams(
            collective_id=0, has_side_effects=True, vmem_limit_bytes=60 << 20
        ),
        cost_estimate=pl.CostEstimate(flops=7_000_000_000, bytes_accessed=20_000_000, transcendentals=131072),
    )(
        qkv, resid, targets, short_filter, long_filter, skip.reshape(1, -1), out_weight,
        gain.reshape(1, -1), vocab_weight,
    )


def solution(mesh):
    in_specs = (
        P("fsdp", "seq", None),
        P("fsdp", "seq", None),
        P("fsdp", "seq"),
        P(),
        P(),
        P(),
        P("fsdp", None),
        P(),
        P("fsdp", None),
    )
    out_specs = P("fsdp", "seq")
    return jax.shard_map(body, mesh=mesh, in_specs=in_specs, out_specs=out_specs, check_vma=False)
```

```python
import jax
import jax.numpy as jnp
from jax import lax
from jax.experimental import pallas as pl
from jax.experimental.pallas import tpu as pltpu
from jax.sharding import PartitionSpec as P

MESH = pl.DeviceIdType.MESH
BF = jnp.bfloat16
F32 = jnp.float32


def place(x, y, z, c):
    x, y, z = lax.rem(x + 4, 4), lax.rem(y + 4, 4), lax.rem(z + 16, 16)
    return (x * 8 + lax.rem(z, 8), (y * 2 + z // 8) * 2 + c)


def cols(start, size):
    return pl.ds(pl.multiple_of(start, 128), size)


def kernel(
    qkv, resid, targets, taps_in, longs_in, skip_in, ow, gain_in, vw, out,
    raw, ext, pack, prod, ferry, query, flips, mats, gated, wbuf, stream, base, taps, longs, skip, gain, wanted,
    local_sem, send_sem, recv_sem, gate_sem,
):
    H = 2048
    s, f = lax.axis_index("seq"), lax.axis_index("fsdp")
    x, zl = s // 8, lax.rem(s, 8)
    y, h, c = f // 4, lax.rem(f // 2, 2), lax.rem(f, 2)
    o = 1 - h
    z = h * 8 + zl
    lo, hi = zl == 0, zl == 7
    edge = jnp.logical_or(lo, hi)
    rank = jnp.where(zl < 5, zl, 7 - zl)
    outward = jnp.where(zl < 5, -1, 1)
    passes = jnp.logical_or(zl < 4, zl > 5)

    def xpeer(d):
        return place(x + d, y, z, c)

    def ypeer(d):
        return place(x, y + d, z, c)

    def back(a, d):
        return lax.rem(a + 4 - d, 4)

    outer, inner = place(x, y, z + outward, c), place(x, y, z - outward, c)
    sibling = (s, f + 1 - 2 * c)
    after, before = (lax.rem(s + 1, 32), f), (lax.rem(s + 31, 32), f)
    around, near = (1, 3, 2), (1, 3)

    barrier = pltpu.get_barrier_semaphore()

    def greet(device):
        pl.semaphore_signal(barrier, inc=1, device_id=device, device_id_type=MESH)

    for d in around:
        greet(xpeer(d))
        greet(ypeer(d))
    for device in (sibling, after, before, outer):
        greet(device)

    @pl.when(passes)
    def _():
        greet(inner)

    far = place(x, y, jnp.where(lo, z + 7, z - 7), c)

    @pl.when(edge)
    def _():
        greet(far)

    guard = zl == 6

    loads = []

    def load(src, dst):
        copy = pltpu.make_async_copy(src, dst, local_sem.at[len(loads)])
        copy.start()
        loads.append(copy)
        return copy

    def own(half, strip):
        at = pl.ds(strip * 512 + half * 256, 256)
        return [
            load(ow.at[:, at], wbuf.at[y, h, c, half, strip, 0:128]),
            load(vw.at[:, at], wbuf.at[y, h, c, half, strip, 128:160]),
        ]

    load_own = [copy for half in (1, 0) for strip in range(4) for copy in own(half, strip)]
    load_late = load(qkv.at[0, 112:256, H:], raw.at[128:272, H:])
    load_taps = load(taps_in, taps)
    load_early = load(qkv.at[0, 0:112, H:], raw.at[16:128, H:])
    load_q = load(qkv.at[0, :, :H], raw.at[16:272, :H])
    load_rest = [
        load(longs_in, longs), load(skip_in, skip), load(gain_in, gain), load(targets, wanted), load(resid.at[0], base),
    ]

    count = [0]

    def send(src, device, dst=None, slot=None):
        n = count[0]
        count[0] += 1
        return pltpu.make_async_remote_copy(
            src_ref=src, dst_ref=src if dst is None else dst, send_sem=send_sem.at[n],
            recv_sem=recv_sem.at[n if slot is None else slot], device_id=device, device_id_type=MESH,
        )

    def strip(yy, hh, half, xx):
        return wbuf.at[yy, hh, c, half, xx]

    def whole(yy, hh, half):
        return wbuf.at[yy, hh, c, half]

    def column(hh, half, xx):
        return wbuf.at[:, hh, c, half, xx]

    def half_whole(yy, hh, d):
        return wbuf.at[yy, hh, c, 0, 0:2] if d == 1 else wbuf.at[yy, hh, c, 0, 2:4]

    def half_column(xx, d):
        return wbuf.at[0:2, o, c, 1, xx] if d == 1 else wbuf.at[2:4, o, c, 1, xx]

    def piece(hh, k):
        return wbuf.at[y, hh, c, k // 2, x, pl.ds(k % 2 * 80, 80)]

    cross, onward = [], []
    for k in range(4):
        slot = count[0]
        cross.append(send(piece(h, k), outer, slot=slot))
        onward.append(send(piece(o, k), inner, slot=slot))
    heads = send(pack.at[0], after, dst=pack.at[1])
    tails, ferry_out, ferry_on = [], [], []
    for k in (0, 1):
        at, slot = pl.ds(k * 1024, 1024), count[0]
        tails.append(send(prod.at[256:384, at], after, dst=prod.at[0:128, at]))
        ferry_out.append(send(prod.at[256:384, at], xpeer(1), dst=ferry.at[k]))
        ferry_on.append(send(ferry.at[k], far, dst=prod.at[0:128, at], slot=slot))
    first = {d: send(strip(y, h, 1, x), ypeer(d)) for d in around}
    second = {(k, d): send(strip(back(y, k), h, 1, x), xpeer(d)) for k in around for d in near}
    second_on = {
        (k, d): send(strip(back(y, k), h, 1, back(x, d)), xpeer(d)) for k, d in ((1, 1), (3, 3))
    }
    for d in near:
        second_on[2, d] = send(wbuf.at[back(y, 2), h, c, 1, back(x, d), pl.ds(d // 2 * 80, 80)], xpeer(d))
    direct = {d: send(whole(y, h, 0), ypeer(d)) for d in near}
    relay = {d: send(half_whole(back(y, d), h, d), ypeer(d)) for d in near}
    spread0 = {d: send(strip(y, o, 0, x), xpeer(d)) for d in around}
    spread1 = {d: send(strip(y, o, 1, x), ypeer(d)) for d in around}
    wide0 = {d: send(whole(y, o, 0), ypeer(d)) for d in near}
    wide1 = {d: send(column(o, 1, x), xpeer(d)) for d in near}
    relay0 = {d: send(half_whole(back(y, d), o, d), ypeer(d)) for d in near}
    relay1 = {d: send(half_column(back(x, d), d), xpeer(d)) for d in near}
    mate = send(wbuf.at[y, h, c], sibling)
    mate_direct = {d: send(whole(back(y, d), h, 0), sibling) for d in around}
    mate_second = {d: send(whole(back(y, d), h, 1), sibling) for d in around}
    mate_wide0 = {d: send(whole(back(y, d), o, 0), sibling) for d in (0,) + near}
    mate_wide1 = {d: send(column(o, 1, back(x, d)), sibling) for d in (0,) + near}
    mate_relay0 = {d: send(half_whole(back(y, 2), o, d), sibling) for d in near}
    mate_relay1 = {d: send(half_column(back(x, 2), d), sibling) for d in near}

    def conv(col, top, spot):
        ext[spot] = raw[top : top + 144, cols(col, 128)].astype(F32)
        total = jnp.zeros((128, 128), F32)
        for lag in range(7):
            total = total + taps[lag : lag + 1, cols(col, 128)] * ext[spot, 16 - lag : 144 - lag]
        return total

    def product(lane, top, spot):
        k = conv(H + lane, top, spot)
        v = conv(2 * H + lane, top, spot + 1)
        prod[128 + top : 256 + top, cols(lane, 128)] = (k * v).astype(BF)

    def late_rows():
        load_late.wait()
        load_taps.wait()
        load_q.wait()
        last = raw[256:272].astype(F32)[8:16]
        pack[0] = jnp.concatenate([last[:, :3072], last[:, 3072:]], axis=0).astype(BF)

        @pl.loop(0, 16)
        def _(j):
            product(j * 128, 128, 0)

    pl.when(hi)(late_rows)
    for copy in load_own:
        copy.wait()
    pl.semaphore_wait(barrier, 10 + jnp.where(passes, 1, 0) + jnp.where(edge, 1, 0))

    @pl.when(edge)
    def _():
        for copy in cross:
            copy.start()

    for d in around:
        first[d].start()
    pl.when(jnp.logical_not(hi))(late_rows)

    def hand_on(*copies):
        for copy in copies:
            copy.start()

    @pl.when(hi)
    def _():
        hand_on(*ferry_out)

    @pl.when(jnp.logical_or(zl == 3, jnp.logical_not(passes)))
    def _():
        hand_on(heads, tails[0])

    @pl.when(jnp.logical_not(passes))
    def _():
        hand_on(tails[1])

    for d in near:
        direct[d].start()
    mate.start()

    def cross_over(level):
        @pl.when(rank == level)
        def _():
            for k in range(4):
                onward[k].wait_recv()
                if level < 4:
                    pl.when(passes)(onward[k].start)
                if k % 2:
                    for d in around:
                        (spread0, spread1)[k // 2][d].start()

    cross_over(0)

    @pl.when(lo)
    def _():
        hand_on(heads, *tails)

    for k in around:
        first[k].wait_recv()
        pl.when(jnp.logical_not(hi))(second[k, 1].start)
        second[k, 3].start()

    cross_over(1)

    @pl.when(rank == 1)
    def _():
        hand_on(heads, *tails)

    rows = lax.broadcasted_iota(jnp.int32, (128, 128), 0)
    lanes = lax.broadcasted_iota(jnp.int32, (128, 128), 1)
    turn = jnp.where(lax.rem(rows + lanes, 128) == 0, 1.0, 0.0).astype(BF)
    load_rest[0].wait()
    flips[...] = jnp.dot(longs[...], turn, preferred_element_type=F32)

    @pl.loop(0, 16)
    def _(j):
        for k in range(8):
            g = j * 8 + k
            spin = pltpu.roll(jnp.broadcast_to(flips[pl.ds(g, 1), :], (128, 128)), 0, 1, stride=1, stride_axis=0)
            at = pl.ds(pl.multiple_of(g * 128, 128), 128)
            mats[at, 0:128] = jnp.where(lanes > rows, spin, 0.0).astype(BF)
            mats[at, 128:256] = jnp.where(lanes > rows, 0.0, spin).astype(BF)

    cross_over(2)

    @pl.when(guard)
    def _():
        for copy in onward:
            copy.wait_send()
        pl.semaphore_signal(gate_sem, inc=1, device_id=outer, device_id_type=MESH)

    @pl.when(zl == 2)
    def _():
        hand_on(heads, *tails)

    cross_over(3)

    @pl.when(zl == 3)
    def _():
        hand_on(tails[1])

    cross_over(4)

    @pl.when(hi)
    def _():
        pl.semaphore_wait(gate_sem, 1)
        hand_on(heads)
        ferry_out[0].wait_recv()
        ferry_on[0].start()

    for d in near:
        direct[d].wait_recv()
        relay[d].start()

    @pl.when(hi)
    def _():
        ferry_out[1].wait_recv()
        ferry_on[1].start()
        for k in around:
            second[k, 1].start()

    for copy in second.values():
        copy.wait_recv()
    for copy in second_on.values():
        copy.start()

    for d in near:
        mate_direct[d].start()
    for copy in second_on.values():
        copy.wait_recv()
    for d in around:
        mate_second[d].start()
    for d in around:
        spread0[d].wait_recv()
    for d in near:
        wide0[d].start()
    for d in around:
        spread1[d].wait_recv()
    for d in near:
        wide1[d].start()
    mate_wide0[0].start()
    mate_wide1[0].start()
    for d in near:
        relay[d].wait_recv()
    mate_direct[2].start()

    def pass_wide():
        for d in near:
            wide0[d].wait_recv()
            relay0[d].start()
            wide1[d].wait_recv()
            relay1[d].start()
        for d in near:
            mate_wide0[d].start()
            mate_wide1[d].start()

    load_early.wait()
    for copy in load_rest[1:]:
        copy.wait()
    heads.wait_recv()
    got = jnp.where(s == 0, 0.0, pack[1].astype(F32))
    raw[0:16, :3072] = jnp.concatenate([got[0:8], got[0:8]], axis=0).astype(BF)
    raw[0:16, 3072:] = jnp.concatenate([got[8:16], got[8:16]], axis=0).astype(BF)

    @pl.loop(0, 16)
    def _(j):
        lane = j * 128
        product(lane, 0, 0)
        query[0:128, cols(lane, 128)] = conv(lane, 0, 2)
        query[128:256, cols(lane, 128)] = conv(lane, 128, 3)

    def pass_relays():
        for d in near:
            relay0[d].wait_recv()
            mate_relay0[d].start()
            relay1[d].wait_recv()
            mate_relay1[d].start()

    @pl.when(lo)
    def _():
        pass_wide()
        pass_relays()

    for copy in tails:
        copy.wait_recv()

    @pl.when(s == 0)
    def _():
        prod[0:128] = jnp.zeros((128, H), BF)

    group = lax.broadcasted_iota(jnp.int32, (128, 128), 1) // 16

    @pl.loop(0, 16, unroll=2)
    def _(j):
        lane = cols(j * 128, 128)
        pair = jnp.concatenate([prod[0:256, lane], prod[128:384, lane]], axis=1)
        spans = jnp.dot(mats[pl.ds(pl.multiple_of(j * 1024, 1024), 1024), :], pair, preferred_element_type=F32)
        for b in (0, 1):
            wave = spans[0:128, b * 128 : b * 128 + 128]
            for g in range(1, 8):
                wave = jnp.where(group == g, spans[g * 128 : g * 128 + 128, b * 128 : b * 128 + 128], wave)
            at = slice(b * 128, b * 128 + 128)
            wave = wave + skip[:, lane] * prod[b * 128 + 128 : b * 128 + 256, lane].astype(F32)
            gated[at, lane] = (query[at, lane] * wave).astype(BF)

    def tile(half, xx):
        return cols(xx * 512 + half * 256, 256)

    def project(hh, half, xx, blocks):
        left = jnp.concatenate([gated[:, cols((yy * 2 + hh) * 256, 256)] for yy in blocks], axis=1)
        right = jnp.concatenate([wbuf[yy, hh, :, half, xx, 0:128, :].reshape(256, 256) for yy in blocks], axis=0)
        return jnp.dot(left, right, preferred_element_type=F32)

    def gather_in(half, xx, blocks):
        at = tile(half, xx)
        stream[:, at] = stream[:, at] + project(o, half, xx, blocks)

    pl.when(jnp.logical_not(lo))(pass_wide)
    mate.wait_recv()
    for d in around:
        mate_direct[d].wait_recv()
    for d in around:
        mate_second[d].wait_recv()

    @pl.loop(0, 8, unroll=2)
    def _(n):
        half, xx = n // 4, lax.rem(n, 4)
        at = tile(half, xx)
        stream[:, at] = base[:, at].astype(F32) + project(h, half, xx, range(4))

    for group_of in (mate_wide0, mate_wide1):
        for copy in group_of.values():
            copy.wait_recv()

    @pl.loop(0, 3, unroll=3)
    def _(n):
        gather_in(1, lax.rem(x + 3 + n, 4), range(4))

    @pl.loop(0, 4, unroll=4)
    def _(n):
        gather_in(0, n, [lax.rem(y + 3 + k, 4) for k in range(3)])

    pl.when(jnp.logical_not(lo))(pass_relays)
    for group_of in (mate_relay0, mate_relay1):
        for copy in group_of.values():
            copy.wait_recv()

    gather_in(1, lax.rem(x + 2, 4), range(4))

    def close(n, squares):
        gather_in(0, n, [lax.rem(y + 2, 4)])
        for half in (0, 1):
            total = stream[:, tile(half, n)]
            squares = squares + total[:, :128] * total[:, :128] + total[:, 128:] * total[:, 128:]
        return squares

    squares = lax.fori_loop(0, 4, close, jnp.zeros((256, 128), F32), unroll=2)
    scale = lax.rsqrt(jnp.sum(squares, axis=1, keepdims=True) / 2048.0 + 1e-05)

    @pl.loop(0, 8, unroll=2)
    def _(n):
        at = cols(n * 256, 256)
        gated[:, at] = (stream[:, at] * scale * gain[:, at]).astype(BF)

    words = jnp.concatenate(
        [wbuf[:, :, :, n % 2, n // 2, 128:160, :].reshape(512, 256) for n in range(8)], axis=1
    )
    logits = lax.dot_general(words, gated[...], (((1,), (1,)), ((), ())), preferred_element_type=F32)
    top = jnp.max(logits, axis=0, keepdims=True)
    total = top + jnp.log(jnp.sum(jnp.exp(logits - top), axis=0, keepdims=True))
    entry = lax.broadcasted_iota(jnp.int32, (512, 256), 0)
    out[...] = jnp.sum(jnp.where(entry == wanted[...], logits, 0.0), axis=0, keepdims=True) - total

    @pl.when(edge)
    def _():
        for copy in cross:
            copy.wait_send()

    @pl.when(jnp.logical_and(passes, jnp.logical_not(guard)))
    def _():
        for copy in onward:
            copy.wait_send()

    @pl.when(hi)
    def _():
        for copy in (*ferry_out, *ferry_on):
            copy.wait_send()

    @pl.when(jnp.logical_not(hi))
    def _():
        for copy in tails:
            copy.wait_send()

    for copy in (heads, mate):
        copy.wait_send()
    for group_of in (
        first, second, second_on, direct, relay, spread0, spread1, wide0, wide1, relay0, relay1, mate_direct, mate_second, mate_wide0, mate_wide1,
        mate_relay0, mate_relay1,
    ):
        for copy in group_of.values():
            copy.wait_send()


def body(qkv, resid, targets, short_filter, long_filter, skip, out_weight, gain, vocab_weight):
    vmem = pl.BlockSpec(memory_space=pltpu.VMEM)
    hbm = pl.BlockSpec(memory_space=pltpu.HBM)
    return pl.pallas_call(
        kernel,
        name="hyena_block",
        out_shape=jax.ShapeDtypeStruct((1, 256), F32),
        in_specs=[hbm] * 9,
        out_specs=vmem,
        scratch_shapes=[
            pltpu.VMEM((272, 6144), BF),
            pltpu.VMEM((4, 144, 128), F32),
            pltpu.VMEM((2, 16, 3072), BF),
            pltpu.VMEM((384, 2048), BF),
            pltpu.VMEM((2, 128, 1024), BF),
            pltpu.VMEM((256, 2048), F32),
            pltpu.VMEM((128, 128), F32),
            pltpu.VMEM((16384, 256), BF),
            pltpu.VMEM((256, 2048), BF),
            pltpu.VMEM((4, 2, 2, 2, 4, 160, 256), BF),
            pltpu.VMEM((256, 2048), F32),
            pltpu.VMEM((256, 2048), BF),
            pltpu.VMEM((7, 6144), F32),
            pltpu.VMEM((128, 128), BF),
            pltpu.VMEM((1, 2048), F32),
            pltpu.VMEM((1, 2048), F32),
            pltpu.VMEM((1, 256), jnp.int32),
            pltpu.SemaphoreType.DMA((32,)),
            pltpu.SemaphoreType.DMA((72,)),
            pltpu.SemaphoreType.DMA((72,)),
            pltpu.SemaphoreType.REGULAR,
        ],
        compiler_params=pltpu.CompilerParams(
            collective_id=0, has_side_effects=True, vmem_limit_bytes=60 << 20
        ),
        cost_estimate=pl.CostEstimate(flops=7_000_000_000, bytes_accessed=20_000_000, transcendentals=131072),
    )(
        qkv, resid, targets, short_filter, long_filter, skip.reshape(1, -1), out_weight,
        gain.reshape(1, -1), vocab_weight,
    )


def solution(mesh):
    in_specs = (
        P("fsdp", "seq", None),
        P("fsdp", "seq", None),
        P("fsdp", "seq"),
        P(),
        P(),
        P(),
        P("fsdp", None),
        P(),
        P("fsdp", None),
    )
    out_specs = P("fsdp", "seq")
    return jax.shard_map(body, mesh=mesh, in_specs=in_specs, out_specs=out_specs, check_vma=False)
```
